256 devices in a mesh: ctx: 64 (over x_lo, y, z), head: 4 (over x_hi, core).
Axes of the slice: x: 4 (x_hi: 2, x_lo: 2; x = x_hi * 2 + x_lo), y: 4, z: 8, core: 2. Of those that a mesh axis runs over, the one named last changes fastest.
Arguments:
- tokens: bfloat16 [16384, 4096], P(('ctx', 'head')), may hold values from -24 to 24
- w_query: bfloat16 [4096, 4096], P(None, 'head'), may hold values from -0.09375 to 0.09375
- w_key: bfloat16 [4096, 512], P(None, 'head'), may hold values from -0.09375 to 0.09375
- w_value: bfloat16 [4096, 512], P(None, 'head'), may hold values from -0.09375 to 0.09375
- block_order: int32 [128], replicated, may hold values from 0 to 127, each once
Outputs:
- attended: bfloat16 [16384, 4096], P('ctx', 'head')
The draws below stay inside these ranges and needn't reach their ends.
All inputs are finite; a program needn't handle non-finite values.
Results may differ from the reference program's by a relative error of at most 0.0075.
The reference program's roundings to bfloat16 on the way count: a program that leaves them out, or rounds other values in their place, can miss the bound.
Values may be sent and summed in bfloat16 or wider, within the bound.
A program may use at most 128 MiB of HBM per device.

```python
import math
import jax
import jax.numpy as jnp
import numpy as np
from jax import lax

D = 4096
HQ = 32
HK = 4
HD = 128
BLK = 128
NBLK = 128
TOKENS = 16384


def draw_tokens(key, part):
    key = jax.random.fold_in(key, 11)
    first = jax.random.fold_in(key, 0)
    values = jax.random.normal(first, (TOKENS, D), jnp.float32)
    return jnp.clip(values, -24.0, 24.0).astype(jnp.bfloat16)


def block_levels(rng, extent, pieces, low, high):
    level = 1.0
    for axis_at, shards_of in pieces:
        draws = jax.random.uniform(jax.random.fold_in(jax.random.fold_in(rng, 6), axis_at), (shards_of,), jnp.float32, low / len(pieces), high / len(pieces))
        level = level * jnp.repeat(jnp.exp(draws), extent[axis_at] // shards_of).reshape((-1,) + (1,) * (len(extent) - 1 - axis_at))
    return level


def gaussian(rng, dims, deviation, reach, pieces=(), kind=jnp.bfloat16):
    factor_of = block_levels(rng, dims, pieces, -0.22, 0.18) if pieces else 1.0
    result = jax.random.normal(rng, dims, jnp.float32) * deviation * factor_of
    return jnp.minimum(jnp.maximum(result, -reach), reach).astype(kind)


def setup_inputs(seed: int = 0) -> dict:
    key_list = jax.random.split(jax.random.key(seed), 6)
    return {
        "tokens": draw_tokens(jax.random.fold_in(key_list[5], 71), 0),
        "w_query": gaussian(key_list[1], (D, HQ * HD), D ** -0.5, 0.09375, ((1, 4),)),
        "w_key": gaussian(key_list[2], (D, HK * HD), D ** -0.5, 0.09375, ((1, 4),)),
        "w_value": gaussian(key_list[3], (D, HK * HD), D ** -0.5, 0.09375, ((1, 4),)),
        "block_order": jax.random.permutation(key_list[4], NBLK).astype(jnp.int32),
    }


def rotary_tables(count):
    half = HD // 2
    freqs = 500000.0 ** (-(np.arange(half) * 2.0) / HD)
    angles = (np.arange(count) * 1.0)[:, None] * freqs[None, :]
    return (jnp.asarray(np.cos(angles), jnp.float32), jnp.asarray(np.sin(angles), jnp.float32))

def rotate(values, cosine, sine, heads):
    count = values.shape[0]
    half = HD // 2
    split = values.reshape(count, heads, HD)
    first = split[:, :, :half]
    second = split[:, :, half:]
    cos_part = cosine[:, None, :]
    sin_part = sine[:, None, :]
    joined = jnp.concatenate([first * cos_part - second * sin_part, second * cos_part + first * sin_part], 2)
    return joined.reshape(count, heads * HD)

def reference(tokens, w_query, w_key, w_value, block_order):
    offsets = jnp.arange(BLK, dtype=jnp.int32)
    position = (block_order[:, None] * BLK + offsets[None, :]).reshape(-1).astype(jnp.int32)
    cos_table, sin_table = rotary_tables(TOKENS)
    cosine = jnp.take(cos_table, position, axis=0)
    sine = jnp.take(sin_table, position, axis=0)
    query = rotate(jnp.dot(tokens, w_query, preferred_element_type=jnp.float32), cosine, sine, HQ).astype(jnp.bfloat16)
    key = rotate(jnp.dot(tokens, w_key, preferred_element_type=jnp.float32), cosine, sine, HK).astype(jnp.bfloat16)
    value = jnp.dot(tokens, w_value, preferred_element_type=jnp.float32).astype(jnp.bfloat16)
    group = HQ // HK
    block_rows = math.gcd(TOKENS, 2048)
    scale = 1.0 / math.sqrt(HD)

    def one_head(head_index):
        query_head = lax.dynamic_slice_in_dim(query, head_index * HD, HD, 1)
        shared = head_index // group
        key_head = lax.dynamic_slice_in_dim(key, shared * HD, HD, 1)
        value_head = lax.dynamic_slice_in_dim(value, shared * HD, HD, 1)

        def one_block(block_index):
            query_rows = lax.dynamic_slice_in_dim(query_head, block_index * block_rows, block_rows, 0)
            query_pos = lax.dynamic_slice_in_dim(position, block_index * block_rows, block_rows, 0)
            scores = jnp.dot(query_rows, key_head.T, preferred_element_type=jnp.float32) * scale
            keep = position[None, :] <= query_pos[:, None]
            scores = jnp.where(keep, scores, -1e+30)
            largest = lax.optimization_barrier(jnp.max(scores, axis=1, keepdims=True))
            expo = jnp.where(keep, jnp.exp(scores - largest), 0.0)
            total = lax.optimization_barrier(jnp.sum(expo, axis=1))
            mixed = jnp.dot(expo.astype(jnp.bfloat16), value_head, preferred_element_type=jnp.float32)
            return (mixed / total[:, None]).astype(jnp.bfloat16)
        blocks = lax.map(one_block, jnp.arange(TOKENS // block_rows, dtype=jnp.int32))
        return blocks.reshape(TOKENS, HD)
    heads_out = lax.map(one_head, jnp.arange(HQ, dtype=jnp.int32))
    return jnp.transpose(heads_out, (1, 0, 2)).reshape(TOKENS, HQ * HD)
```

```python
import math

import jax
import jax.numpy as jnp
import numpy as np
from jax import lax
from jax.experimental import pallas as pl
from jax.experimental.pallas import tpu as pltpu
from jax.sharding import PartitionSpec as P

HD = 128
BLK = 128
NX, NY, NZ = 2, 4, 8
STEPS = 16
PAIRS = 4
TILE = 256
LOW = -1e30
FACTOR = math.log2(math.e) / math.sqrt(HD)
CONTRACT_LAST = (((1,), (1,)), ((), ()))
MOVES = {"x": (1, 0, 0), "y+": (0, 1, 0), "y-": (0, -1, 0), "z+": (0, 0, 1), "z-": (0, 0, -1)}


def moved(item, way):
    kind, x, y, z = item
    dx, dy, dz = MOVES[way]
    return (kind, (x + dx) % NX, (y + dy) % NY, (z + dz) % NZ)


def all_messages():
    out = [("x", (("E", 0, 0, 0),)), ("x", (("L", 0, 0, 0),))]

    def pair(kind, y, z):
        return ((kind, 0, y, z), (kind, 1, y, z))

    for x in range(NX):
        out += [("z+", (("E", x, 0, 0),)), ("z-", (("E", x, 0, 0),))]
    out += [("z+", pair("E", 0, 1)), ("z+", pair("E", 0, 2))]
    out += [("z-", pair("E", 0, 7)), ("z-", pair("E", 0, 6))]
    out += [("z+", (("E", 0, 0, 3),)), ("z-", (("E", 1, 0, 5),))]
    for z in range(NZ):
        out += [("y+", pair("E", 0, z)), ("y-", pair("E", 0, z))]
        out += [("y+", pair("E", 1, z)) if z % 2 == 0 else ("y-", pair("E", 3, z))]
    out += [("y+", pair("L", 0, 0)), ("y-", pair("L", 0, 0))]
    out += [("y+", (("L", 0, 1, 0),)), ("y-", (("L", 1, 3, 0),))]
    for y in range(NY):
        for z in (0, 1, 2):
            out += [("z+", pair("L", y, z)), ("z-", pair("L", y, -z % NZ))]
        out += [("z+", pair("L", y, 3)) if y % 2 == 0 else ("z-", pair("L", y, 5))]
    return out


def plan():
    messages = all_messages()
    block_us, latency = 1.42, 2.4
    segments = [("qE", 0.8)] * 4 + [("kvL", 1.0)] + [("qL", 0.8)] * 4 + [("own", 0.6)]
    segments += [("step", 3.0)] * STEPS
    have = {("E", 0, 0, 0)}
    free = {way: 0.0 for way in MOVES}
    arrival, unsent, arrived, used = {}, list(range(len(messages))), set(), set()
    now = 4.0
    actions, order = [], []

    def send_ready(acts):
        for m in list(unsent):
            way, items = messages[m]
            if all(item in have for item in items):
                unsent.remove(m)
                free[way] = max(now, free[way]) + block_us * len(items)
                arrival[m] = free[way] + latency
                acts.append(("send", m))

    def take(m, acts):
        nonlocal now
        acts.append(("wait", m))
        now = max(now, arrival[m])
        arrived.add(m)
        have.update(moved(item, messages[m][0]) for item in messages[m][1])
        send_ready(acts)

    def pending():
        return sorted((arrival[m], m) for m in arrival if m not in arrived)

    def ready_pairs():
        return [
            (k, y, z)
            for k, x, y, z in sorted(have, key=lambda item: when.get(item, 0.0))
            if x == 0 and (k, 1, y, z) in have and (k, y, z) not in used
        ]

    when = {}
    for what, length in segments:
        acts = []
        if what == "kvL":
            now = max(now, 13.0)
        send_ready(acts)
        while True:
            soon = [(t, m) for t, m in pending() if t <= now]
            if not soon:
                break
            take(soon[0][1], acts)
        if what == "step":
            while len(ready_pairs()) < PAIRS:
                take(pending()[0][1], acts)
            chosen = ready_pairs()[:PAIRS]
            used.update(chosen)
            order.append(chosen)
        actions.append((what, acts))
        now += length
        if what == "kvL":
            have.add(("L", 0, 0, 0))
    assert len(arrived) == len(messages)
    place = {
        (k, x, y, z): (step, p * NX + x)
        for step, chosen in enumerate(order)
        for p, (k, y, z) in enumerate(chosen)
        for x in range(NX)
    }
    assert len(place) == 2 * NX * NY * NZ
    return messages, actions, place, now


MESSAGES, ACTIONS, PLACE, ESTIMATE = plan()


def kernel(
    tok_in, wq_in, wk_in, wv_in, table, aug, out,
    tok, wq, wkv, query, kv, largest, acc,
    send, recv, tok_sem, relay_sem, local,
):
    ctx, head = lax.axis_index("ctx"), lax.axis_index("head")
    x, y, z = ctx // 32, (ctx // 8) % 4, ctx % 8
    core = head % 2

    def device(x, y, z):
        return ((x * 4 + y) * 8 + z, head)

    near = {
        "x": device(1 - x, y, z),
        "y+": device(x, (y + 1) % 4, z),
        "y-": device(x, (y + 3) % 4, z),
        "z+": device(x, y, (z + 1) % 8),
        "z-": device(x, y, (z + 7) % 8),
    }
    beside = (ctx, head + 1 - 2 * core)
    across = (ctx, (head + 2) % 4)

    copies = [
        pltpu.make_async_copy(wk_in, wkv.at[:, 0:HD], local.at[0]),
        pltpu.make_async_copy(wv_in, wkv.at[:, HD : 2 * HD], local.at[1]),
    ]
    mine = pl.ds(pl.multiple_of(core * 64, 64), 64)
    own_tokens = pltpu.make_async_copy(tok_in, tok.at[0, mine], local.at[2])
    own_tokens.start()
    for copy in copies:
        copy.start()
    wide = []
    for j in range(4):
        columns = pl.ds(j * TILE, TILE)
        wide.append(pltpu.make_async_copy(wq_in.at[:, columns], wq.at[:, columns], local.at[3 + j]))
        wide[-1].start()

    barrier = pltpu.get_barrier_semaphore()
    peers = list(near.values()) + [beside, across]
    for peer in peers:
        pl.semaphore_signal(barrier, inc=1, device_id=peer, device_id_type=pl.DeviceIdType.MESH)
    pl.semaphore_wait(barrier, len(peers))

    def remote(src, dst, s, r, to):
        return pltpu.make_async_remote_copy(
            src_ref=src, dst_ref=dst, send_sem=s, recv_sem=r, device_id=to,
            device_id_type=pl.DeviceIdType.MESH,
        )

    to_beside = remote(tok_in, tok.at[0, mine], tok_sem.at[0], tok_sem.at[1], beside)
    to_beside.start()
    to_across, relays = [], []
    for j in range(4):
        rows = pl.ds(pl.multiple_of(core * 64 + j * 16, 16), 16)
        to_across.append(
            remote(tok_in.at[pl.ds(j * 16, 16)], tok.at[1, rows], tok_sem.at[2 + j], tok_sem.at[6 + j], across)
        )
        to_across[-1].start()
        relays.append(
            remote(tok.at[1, rows], tok.at[1, rows], relay_sem.at[j], relay_sem.at[4 + j], beside)
        )

    def slot(items):
        step, p = PLACE[items[0]]
        return kv.at[step, :, pl.ds(p * BLK, BLK * len(items))]

    def message(m):
        way, items = MESSAGES[m]
        landing = [moved(item, way) for item in items]
        landing.sort(key=lambda item: PLACE[item])
        taking = sorted(items, key=lambda item: PLACE[item])
        assert len(items) == 1 or way != "x"
        return remote(slot(taking), slot(landing), send.at[m], recv.at[m], near[way])

    def communicate(acts):
        for what, m in acts:
            if what == "send":
                message(m).start()
            else:
                message(m).wait_recv()

    def rotated(values, part):
        pieces = table[part]
        swapped = pltpu.roll(pieces, HD // 2, 1)
        first = lax.broadcasted_iota(jnp.int32, pieces.shape, 1) < HD // 2
        cosine = jnp.where(first, pieces, swapped)
        sine = jnp.where(first, -swapped, pieces)
        return (values * cosine + pltpu.roll(values, HD // 2, 1) * sine).astype(jnp.bfloat16)

    def project_kv(part, kind):
        both = jnp.dot(tok[part], wkv[...], preferred_element_type=jnp.float32)
        step, p = PLACE[(kind, 0, 0, 0)]
        rows = pl.ds(p * BLK, BLK)
        kv[step, 0, rows] = rotated(both[:, :HD], part)
        kv[step, 1, rows] = both[:, HD:].astype(jnp.bfloat16)

    def project_q(part, j):
        both = jnp.dot(tok[part], wq[:, j * TILE : (j + 1) * TILE], preferred_element_type=jnp.float32)
        for h in range(2):
            rows = pl.ds(part * 1024 + (2 * j + h) * BLK, BLK)
            query[rows] = rotated(both[:, h * HD : (h + 1) * HD], part)

    lane = lax.broadcasted_iota(jnp.int32, (TILE, HD), 1)
    marks = [jnp.where(lane == part, 1.0, 0.0).astype(jnp.bfloat16) for part in range(2)]

    def own_blocks():
        ones = jnp.ones((BLK, HD), jnp.bfloat16)
        row = lax.broadcasted_iota(jnp.int32, (TILE, BLK), 0) % BLK
        keep = lax.broadcasted_iota(jnp.int32, (TILE, BLK), 1) <= row
        for part, kind in enumerate("EL"):
            step, p = PLACE[(kind, 0, 0, 0)]
            keys = kv[step, 0, pl.ds(p * BLK, BLK)]
            values = jnp.concatenate([kv[step, 1, pl.ds(p * BLK, BLK)], ones], 1)
            for t in range(4):
                rows = pl.ds(part * 1024 + t * TILE, TILE)
                scores = lax.dot_general(query[rows], keys, CONTRACT_LAST, preferred_element_type=jnp.float32)
                scores = jnp.where(keep, scores, LOW)
                top = jnp.broadcast_to(jnp.max(scores, axis=1, keepdims=True), (TILE, HD))
                expo = jnp.exp2((scores - top) * FACTOR).astype(jnp.bfloat16)
                largest[rows] = top
                acc[rows] = jnp.dot(expo, values, preferred_element_type=jnp.float32)

    def attend(step):
        masks = [
            jnp.concatenate([aug[step, b]] * (BLK // 16), 0) for b in range(2 * PAIRS)
        ]
        keys = jnp.concatenate([kv[step, 0], jnp.concatenate(masks, 0)], 1)
        values = jnp.concatenate([kv[step, 1], jnp.ones((1024, HD), jnp.bfloat16)], 1)
        for t in range(8):
            rows = pl.ds(t * TILE, TILE)
            wide_query = jnp.concatenate([query[rows], marks[t // 4]], 1)
            scores = lax.dot_general(wide_query, keys, CONTRACT_LAST, preferred_element_type=jnp.float32)
            before = largest[rows]
            after = jnp.maximum(before, jnp.max(scores, axis=1, keepdims=True))
            largest[rows] = after
            expo = jnp.concatenate(
                [jnp.exp2((scores[:, b * HD : (b + 1) * HD] - after) * FACTOR).astype(jnp.bfloat16) for b in range(8)], 1
            )
            shrink = jnp.exp2((before - after) * FACTOR)
            product = jnp.dot(expo, values, preferred_element_type=jnp.float32)
            acc[rows] = acc[rows] * jnp.concatenate([shrink, shrink], 1) + product

    own_tokens.wait()
    to_beside.wait_recv()
    for copy in copies:
        copy.wait()
    project_kv(0, "E")
    step_acts = []
    j = {"qE": 0, "qL": 0}
    for what, acts in ACTIONS:
        if what == "step":
            step_acts.append(acts)
            continue
        communicate(acts)
        if what == "qE":
            wide[j[what]].wait()
            project_q(0, j[what])
            j[what] += 1
        elif what == "kvL":
            for k in range(4):
                to_across[k].wait_recv()
                relays[k].start()
            for k in range(4):
                relays[k].wait_recv()
            project_kv(1, "L")
        elif what == "qL":
            project_q(1, j[what])
            j[what] += 1
        else:
            own_blocks()

    def one_step(step, carry):
        for s, acts in enumerate(step_acts):
            if acts:

                @pl.when(step == s)
                def _(acts=acts):
                    communicate(acts)

        attend(step)
        return carry

    lax.fori_loop(0, STEPS, one_step, 0)

    early = head // 2
    for part in range(2):
        block = pl.ds(pl.multiple_of((early if part == 0 else 1 - early) * BLK, BLK), BLK)
        for h in range(8):
            rows = pl.ds(part * 1024 + h * BLK, BLK)
            total = acc[rows]
            out[block, h * HD : (h + 1) * HD] = (total[:, :HD] / total[:, HD:]).astype(jnp.bfloat16)

    for m in range(len(MESSAGES)):
        message(m).wait_send()
    to_beside.wait_send()
    for k in range(4):
        to_across[k].wait_send()
        relays[k].wait_send()


def rotary_table(count):
    half = HD // 2
    freqs = 500000.0 ** (-(np.arange(half) * 2.0) / HD)
    angles = (np.arange(count) * 1.0)[:, None] * freqs[None, :]
    joined = np.concatenate([np.cos(angles), np.sin(angles)], 1)
    return jnp.asarray(joined.reshape(count // BLK, BLK, HD), jnp.float32)


def origins():
    inverse = {where: item for item, where in PLACE.items()}
    rows = []
    for step in range(STEPS):
        for b in range(2 * PAIRS):
            kind, x, y, z = inverse[(step, b)]
            rows.append((0 if kind == "E" else 1, x, y, z))
    return np.asarray(rows, np.int32)


def per_device(tokens, w_query, w_key, w_value, block_order):
    ctx, head = lax.axis_index("ctx"), lax.axis_index("head")
    early = head // 2
    x, y, z = ctx // 32, (ctx // 8) % 4, ctx % 8
    rel = origins()
    from_ctx = (((x - rel[:, 1]) % 2) * 4 + (y - rel[:, 2]) % 4) * 8 + (z - rel[:, 3]) % 8
    index = from_ctx * 2 + (rel[:, 0] + early) % 2
    blocks = jnp.arange(128, dtype=jnp.int32)
    place = jnp.sum(jnp.where(index[:, None] == blocks[None, :], block_order[None, :], 0), 1)
    own = [lax.dynamic_index_in_dim(block_order, ctx * 2 + (part + early) % 2, 0, False) for part in range(2)]
    lanes = jnp.arange(HD, dtype=jnp.int32)[None, :]
    bound = jnp.where(lanes == 0, own[0], jnp.where(lanes == 1, own[1], 1 << 20))
    aug = jnp.where(place[:, None] < bound, 0.0, LOW).astype(jnp.bfloat16)
    aug = jnp.broadcast_to(aug[:, None, :], (128, 16, HD)).reshape(STEPS, 2 * PAIRS, 16, HD)
    table = rotary_table(16384)
    table = jnp.concatenate([lax.dynamic_slice_in_dim(table, b, 1, 0) for b in own], 0)
    anywhere, vmem = pl.BlockSpec(memory_space=pl.ANY), pl.BlockSpec(memory_space=pltpu.VMEM)
    count = len(MESSAGES)
    return pl.pallas_call(
        kernel,
        out_shape=jax.ShapeDtypeStruct((256, 1024), jnp.bfloat16),
        in_specs=[anywhere] * 4 + [vmem] * 2,
        out_specs=vmem,
        scratch_shapes=[
            pltpu.VMEM((2, 128, 4096), jnp.bfloat16),
            pltpu.VMEM((4096, 1024), jnp.bfloat16),
            pltpu.VMEM((4096, 256), jnp.bfloat16),
            pltpu.VMEM((2048, HD), jnp.bfloat16),
            pltpu.VMEM((STEPS, 2, 1024, HD), jnp.bfloat16),
            pltpu.VMEM((2048, HD), jnp.float32),
            pltpu.VMEM((2048, 2 * HD), jnp.float32),
            pltpu.SemaphoreType.DMA((count,)),
            pltpu.SemaphoreType.DMA((count,)),
            pltpu.SemaphoreType.DMA((10,)),
            pltpu.SemaphoreType.DMA((8,)),
            pltpu.SemaphoreType.DMA((7,)),
        ],
        compiler_params=pltpu.CompilerParams(
            collective_id=0, has_side_effects=True, vmem_limit_bytes=56 << 20
        ),
        cost_estimate=pl.CostEstimate(flops=38 * 10**9, bytes_accessed=12 * 10**6, transcendentals=33 * 10**6),
    )(tokens, w_query, w_key, w_value, table, aug)


def solution(mesh):
    return jax.shard_map(
        per_device,
        mesh=mesh,
        in_specs=(P(("ctx", "head"), None), P(None, "head"), P(None, "head"), P(None, "head"), P()),
        out_specs=P("ctx", "head"),
        check_vma=False,
    )
```

```python
import math

import jax
import jax.numpy as jnp
import numpy as np
from jax import lax
from jax.experimental import pallas as pl
from jax.experimental.pallas import tpu as pltpu
from jax.sharding import PartitionSpec as P

HD = 128
BLK = 128
NX, NY, NZ = 2, 4, 8
CHUNKS = 16
ROWS = 1024
HALF = 64
TILE = 512
WIDE = 256
AHEAD = 1
LOW = -1e30
FACTOR = math.log2(math.e) / math.sqrt(HD)
CONTRACT_LAST = (((1,), (1,)), ((), ()))
MOVES = {"x": (1, 0, 0), "y+": (0, 1, 0), "y-": (0, -1, 0), "z+": (0, 0, 1), "z-": (0, 0, -1)}
KINDS = {"E": ("E1", "E2"), "L": ("L1", "L2")}
YS = (0, 1, 3, 2)
ZS = (0, 1, 7, 2, 6, 3, 5, 4)
BACKLOG = 3.0
PATHS = {"E1": "xzy", "E2": "zyx", "L1": "yzx", "L2": "xzy"}
FIRST = [
    ("L1", "y"), ("L2", "x"), ("E2", "z"), ("E1", "z"), ("E2", "y"), ("L1", "x"),
    ("L1", "z"), ("L2", "y"), ("E2", "x"), ("E1", "y"), ("L2", "z"), ("E1", "x"),
]


def moved(item, way):
    kind, x, y, z = item
    dx, dy, dz = MOVES[way]
    return (kind, (x + dx) % NX, (y + dy) % NY, (z + dz) % NZ)


def run(kind, xs, ys, zs):
    return [(kind, x, y, z) for y in ys for z in zs for x in xs]


def all_groups():
    out = []
    for kind, path in PATHS.items():
        sides = [(0, 1)] if path[0] == "x" else [(0,), (1,)]
        for xs in sides:
            if path.index("y") < path.index("z"):
                for z in range(NZ):
                    out += [run(kind, xs, ys, (z,)) for ys in (YS[:2], YS[2:])]
            else:
                for y in range(NY):
                    out += [run(kind, xs, (y,), ZS[n : n + 2]) for n in (0, 2, 4, 6)]
    return out


def first_y(kind, xs):
    out = [(way, run(kind, (x,), (0,), (0,))) for x in xs for way in ("y+", "y-")]
    out.append(("y+", run(kind, (0,), (1,), (0,))))
    return out + ([("y-", run(kind, (1,), (3,), (0,)))] if len(xs) > 1 else [])


def first_z(kind, xs):
    out = [(way, run(kind, (x,), (0,), (0,))) for x in xs for way in ("z+", "z-")]
    for up, down in ((1, 7), (2, 6)):
        out += [("z+", run(kind, xs, (0,), (up,))), ("z-", run(kind, xs, (0,), (down,)))]
    out.append(("z+", run(kind, (0,), (0,), (3,))))
    return out + ([("z-", run(kind, (1,), (0,), (5,)))] if len(xs) > 1 else [])


def along_z(kind, xs):
    out = []
    for up, down in ((0, 0), (1, 7), (2, 6)):
        for ys in (YS[:1], YS[1:2], YS[2:]):
            out += [("z+", run(kind, xs, ys, (up,))), ("z-", run(kind, xs, ys, (down,)))]
    out.append(("z+", run(kind, xs, YS[:2], (3,))))
    return out + [("z-", run(kind, xs, YS[2:], (5,)))]


def along_y(kind, xs):
    out = []
    for zs in (ZS[:1], ZS[1:2], ZS[2:4], ZS[4:6], ZS[6:]):
        out += [(way, run(kind, xs, (0,), zs)) for way in ("y+", "y-")]
    for zs in (ZS[:2], ZS[2:4]):
        out.append(("y+", run(kind, xs, (1,), zs)))
    for zs in (ZS[4:6], ZS[6:]):
        out.append(("y-", run(kind, xs, (3,), zs)))
    return out


def stages(kind):
    path, both = PATHS[kind], (0, 1)
    xs = both if path[0] == "x" else (0,)
    if path.index("y") < path.index("z"):
        first, then = ("y", first_y(kind, xs)), ("z", along_z(kind, xs))
        rows = [run(kind, (0,), ys, (z,)) for z in ZS for ys in (YS[:2], YS[2:])]
    else:
        first, then = ("z", first_z(kind, xs)), ("y", along_y(kind, xs))
        rows = [run(kind, (0,), (y,), ZS[n : n + 2]) for y in YS for n in (0, 2, 4, 6)]
    if path[0] == "x":
        rows = [run(kind, (0,), (0,), (0,))]
    return dict([first, then, ("x", [("x", items) for items in rows])])


def all_messages():
    return [message for kind, axis in FIRST for message in stages(kind)[axis]]


def plan():
    messages, groups = all_messages(), all_groups()
    half_us, latency = 0.71, 2.8
    segments = [("qE", 0.6)] * 4 + [("ownE", 0.4)] + [("ahead", 1.25)] * AHEAD
    segments += [("kvL", 0.8)] + [("qL", 0.6)] * 4 + [("ownL", 0.4)]
    segments += [("step", 2.5)] * (CHUNKS - AHEAD)
    have = {("E1", 0, 0, 0), ("E2", 0, 0, 0)}
    free = {way: 0.0 for way in MOVES}
    arrival, unsent, arrived, left = {}, list(range(len(messages))), set(), list(range(len(groups)))
    complete = {}
    now = 2.5
    actions, order = [], []

    def send_ready(acts):
        for m in list(unsent):
            way, items = messages[m]
            if free[way] <= now + BACKLOG and all(item in have for item in items):
                unsent.remove(m)
                free[way] = max(now, free[way]) + half_us * len(items)
                arrival[m] = free[way] + latency
                acts.append(("send", m))

    def note():
        for g in left:
            if g not in complete and all(item in have for item in groups[g]):
                complete[g] = len(complete)

    def take(m, acts):
        nonlocal now
        acts.append(("wait", m))
        now = max(now, arrival[m])
        arrived.add(m)
        have.update(moved(item, messages[m][0]) for item in messages[m][1])
        note()
        send_ready(acts)

    def pending():
        return sorted((arrival[m], m) for m in arrival if m not in arrived)

    def choose(ready, room):
        if room == 0:
            return []
        for n, g in enumerate(ready):
            if len(groups[g]) <= room:
                rest = choose(ready[n + 1 :], room - len(groups[g]))
                if rest is not None:
                    return [g] + rest
        return None

    def chosen_now():
        ready = sorted((g for g in left if g in complete), key=complete.get)
        return choose(ready, ROWS // HALF) if sum(len(groups[g]) for g in ready) >= ROWS // HALF else None

    for what, length in segments:
        acts = []
        if what == "kvL":
            now = max(now, 16.0)
        send_ready(acts)
        while True:
            soon = [(t, m) for t, m in pending() if t <= now]
            if not soon:
                break
            take(soon[0][1], acts)
        if what in ("step", "ahead"):
            while (chosen := chosen_now()) is None:
                take(pending()[0][1], acts)
            for g in chosen:
                left.remove(g)
            order.append(chosen)
        actions.append((what, acts))
        now += length
        if what == "kvL":
            have.update([("L1", 0, 0, 0), ("L2", 0, 0, 0)])
    assert not left and len(arrived) == len(messages)
    place = {}
    for chunk, chosen in enumerate(order):
        row = 0
        for g in chosen:
            for item in groups[g]:
                place[item] = (chunk, row)
                row += HALF
        assert row == ROWS
    return messages, actions, place, now


MESSAGES, ACTIONS, PLACE, ESTIMATE = plan()


def kernel(
    tok_in, wq_in, wk_in, wv_in, blocks, base, offset, out,
    tok, wq, wkv, query, kv, aug, largest, acc,
    send, recv, tok_sem, relay_sem, local,
):
    ctx, head = lax.axis_index("ctx"), lax.axis_index("head")
    x, y, z = ctx // 32, (ctx // 8) % 4, ctx % 8
    early, core = head // 2, head % 2

    def device(x, y, z):
        return ((x * 4 + y) * 8 + z, head)

    near = {
        "x": device(1 - x, y, z),
        "y+": device(x, (y + 1) % 4, z),
        "y-": device(x, (y + 3) % 4, z),
        "z+": device(x, y, (z + 1) % 8),
        "z-": device(x, y, (z + 7) % 8),
    }
    beside = (ctx, head + 1 - 2 * core)
    across = (ctx, (head + 2) % 4)

    barrier = pltpu.get_barrier_semaphore()
    peers = list(near.values()) + [beside, across]
    for peer in peers:
        pl.semaphore_signal(barrier, inc=1, device_id=peer, device_id_type=pl.DeviceIdType.MESH)

    mine = pl.ds(pl.multiple_of(core * 64, 64), 64)
    own_tokens = pltpu.make_async_copy(tok_in, tok.at[0, mine], local.at[2])
    own_tokens.start()
    copies = [
        pltpu.make_async_copy(wk_in, wkv.at[:, 0:HD], local.at[0]),
        pltpu.make_async_copy(wv_in, wkv.at[:, HD : 2 * HD], local.at[1]),
    ]
    for copy in copies:
        copy.start()
    wide = []
    for j in range(4):
        columns = pl.ds(j * WIDE, WIDE)
        wide.append(pltpu.make_async_copy(wq_in.at[:, columns], wq.at[:, columns], local.at[3 + j]))
        wide[-1].start()
    pl.semaphore_wait(barrier, len(peers))

    def remote(src, dst, s, r, to):
        return pltpu.make_async_remote_copy(
            src_ref=src, dst_ref=dst, send_sem=s, recv_sem=r, device_id=to,
            device_id_type=pl.DeviceIdType.MESH,
        )

    to_beside = remote(tok_in, tok.at[0, mine], tok_sem.at[0], tok_sem.at[1], beside)
    to_beside.start()
    to_across, relays = [], []
    for j in range(4):
        rows = pl.ds(pl.multiple_of(core * 64 + j * 16, 16), 16)
        to_across.append(
            remote(tok_in.at[pl.ds(j * 16, 16)], tok.at[1, rows], tok_sem.at[2 + j], tok_sem.at[6 + j], across)
        )
        relays.append(
            remote(tok.at[1, rows], tok.at[1, rows], relay_sem.at[j], relay_sem.at[4 + j], beside)
        )

    to_across[0].start()

    own = [blocks[ctx * 2 + early], blocks[ctx * 2 + 1 - early]]
    lanes = lax.broadcasted_iota(jnp.int32, (16, HD), 1)
    bound = jnp.where(lanes == 0, own[0], jnp.where(lanes == 1, own[1], 1 << 20))
    for dx in range(NX):
        for dy in range(NY):
            for dz in range(NZ):
                origin = (((x + dx) % NX) * 4 + (y - dy + NY) % NY) * 8 + (z - dz + NZ) % NZ
                for part, kinds in ((early, KINDS["E"]), (1 - early, KINDS["L"])):
                    place = blocks[origin * 2 + part]
                    mask = jnp.where(place < bound, 0.0, LOW).astype(jnp.bfloat16)
                    for kind in kinds:
                        chunk, row = PLACE[(kind, dx, dy, dz)]
                        aug[chunk, row // HALF] = mask

    def slot(items):
        chunk, row = PLACE[items[0]]
        count = len(items) * HALF
        spots = [PLACE[item] for item in items]
        assert spots == [(chunk, row + n * HALF) for n in range(len(items))]
        return kv.at[chunk, :, pl.ds(row, count)]

    def message(m):
        way, items = MESSAGES[m]
        landing = [moved(item, way) for item in items]
        return remote(slot(items), slot(landing), send.at[m], recv.at[m], near[way])

    def communicate(acts):
        for what, m in acts:
            if what == "send":
                message(m).start()
            else:
                message(m).wait_recv()

    def rotation(part):
        turn = own[part]
        base_cos, base_sin = base[0, pl.ds(turn, 1)], base[1, pl.ds(turn, 1)]
        cosine = base_cos * offset[0] - base_sin * offset[1]
        sine = base_sin * offset[0] + base_cos * offset[1]
        return lambda values: (values * cosine + pltpu.roll(values, HD // 2, 1) * sine).astype(jnp.bfloat16)

    def project_kv(part, spots):
        both = jnp.dot(tok[part], wkv[...], preferred_element_type=jnp.float32)
        keys, values = rotation(part)(both[:, :HD]), both[:, HD:].astype(jnp.bfloat16)
        size = BLK // len(spots)
        for n, item in enumerate(spots):
            chunk, row = PLACE[item]
            kv[chunk, 0, pl.ds(row, size)] = keys[n * size : (n + 1) * size]
            kv[chunk, 1, pl.ds(row, size)] = values[n * size : (n + 1) * size]

    def project_q(part, j):
        both = jnp.dot(tok[part], wq[:, j * WIDE : (j + 1) * WIDE], preferred_element_type=jnp.float32)
        rotate = rotation(part)
        for h in range(2):
            rows = pl.ds(part * ROWS + (2 * j + h) * BLK, BLK)
            query[rows] = rotate(both[:, h * HD : (h + 1) * HD])

    lane = lax.broadcasted_iota(jnp.int32, (TILE, HD), 1)
    marks = [jnp.where(lane == part, 1.0, 0.0).astype(jnp.bfloat16) for part in range(2)]

    def own_block(part, spots):
        ones = jnp.ones((BLK, HD), jnp.bfloat16)
        row = lax.broadcasted_iota(jnp.int32, (TILE, BLK), 0) % BLK
        keep = lax.broadcasted_iota(jnp.int32, (TILE, BLK), 1) <= row
        size = BLK // len(spots)
        at = [PLACE[item] for item in spots]
        keys, values = (
            jnp.concatenate([kv[chunk, n, pl.ds(row, size)] for chunk, row in at], 0) for n in range(2)
        )
        values = jnp.concatenate([values, ones], 1)
        for t in range(ROWS // TILE):
            rows = pl.ds(part * ROWS + t * TILE, TILE)
            scores = lax.dot_general(query[rows], keys, CONTRACT_LAST, preferred_element_type=jnp.float32)
            scores = jnp.where(keep, scores, LOW)
            top = jnp.broadcast_to(jnp.max(scores, axis=1, keepdims=True), (TILE, HD))
            expo = jnp.exp2((scores - top) * FACTOR).astype(jnp.bfloat16)
            largest[rows] = top
            acc[rows] = jnp.dot(expo, values, preferred_element_type=jnp.float32)

    def score(part, rows, chunk):
        masks = [aug[chunk, b] for b in range(ROWS // HALF) for _ in range(HALF // 16)]
        keys = jnp.concatenate([kv[chunk, 0], jnp.concatenate(masks, 0)], 1)
        wide_query = jnp.concatenate([query[rows], marks[part]], 1)
        return lax.dot_general(wide_query, keys, CONTRACT_LAST, preferred_element_type=jnp.float32)

    def weigh(rows, scores):
        before = largest[rows]
        after = jnp.maximum(before, jnp.max(scores, axis=1, keepdims=True))
        largest[rows] = after
        expo = [
            jnp.exp2((scores[:, n : n + HD] - after) * FACTOR).astype(jnp.bfloat16) for n in range(0, ROWS, HD)
        ]
        return jnp.concatenate(expo, 1), jnp.exp2((before - after) * FACTOR)

    def gather(rows, chunk, expo, shrink):
        values = jnp.concatenate([kv[chunk, 1], jnp.ones((ROWS, HD), jnp.bfloat16)], 1)
        product = jnp.dot(expo, values, preferred_element_type=jnp.float32)
        acc[rows] = acc[rows] * jnp.concatenate([shrink, shrink], 1) + product

    def attend(pairs):
        work = [
            (part, pl.ds(part * ROWS + t * TILE, TILE), chunk) for part, chunk in pairs for t in range(ROWS // TILE)
        ]
        scores, weights = {}, {}
        for n in range(len(work) + 2):
            if n < len(work):
                scores[n] = score(*work[n])
            if n >= 2:
                part, rows, chunk = work[n - 2]
                gather(rows, chunk, *weights.pop(n - 2))
            if 1 <= n <= len(work):
                weights[n - 1] = weigh(work[n - 1][1], scores.pop(n - 1))

    own_tokens.wait()
    to_beside.wait_recv()
    for copy in copies:
        copy.wait()
    spots = [[(kind, 0, 0, 0) for kind in KINDS[part]] for part in "EL"]
    project_kv(0, spots[0])
    step_acts = []
    count = {what: 0 for what, _ in ACTIONS}
    for what, acts in ACTIONS:
        n = count[what]
        count[what] += 1
        if what == "step":
            step_acts.append(acts)
            continue
        communicate(acts)
        if what == "qE" and n == 0:
            for k in range(1, 4):
                to_across[k].start()
        if what == "qE":
            wide[n].wait()
            project_q(0, n)
        elif what == "ownE":
            own_block(0, spots[0])
        elif what == "ahead":
            attend([(0, n)])
        elif what == "kvL":
            for k in range(4):
                to_across[k].wait_recv()
                relays[k].start()
            for k in range(4):
                relays[k].wait_recv()
            project_kv(1, spots[1])
        elif what == "qL":
            project_q(1, n)
        else:
            own_block(1, spots[1])

    def one_step(step, carry):
        for s, acts in enumerate(step_acts):
            if acts:

                @pl.when(step == s)
                def _(acts=acts):
                    communicate(acts)

        attend([(1, step), (0, step + AHEAD)])
        return carry

    lax.fori_loop(0, CHUNKS - AHEAD, one_step, 0)
    attend([(1, chunk) for chunk in range(CHUNKS - AHEAD, CHUNKS)])

    for part in range(2):
        block = pl.ds(pl.multiple_of((early if part == 0 else 1 - early) * BLK, BLK), BLK)
        for h in range(8):
            rows = pl.ds(part * ROWS + h * BLK, BLK)
            total = acc[rows]
            out[block, h * HD : (h + 1) * HD] = (total[:, :HD] / total[:, HD:]).astype(jnp.bfloat16)

    for m in range(len(MESSAGES)):
        message(m).wait_send()
    to_beside.wait_send()
    for k in range(4):
        to_across[k].wait_send()
        relays[k].wait_send()


def rotary_tables():
    freqs = 500000.0 ** (-(np.arange(HD // 2) * 2.0) / HD)
    out = []
    for positions in (np.arange(128.0) * BLK, np.arange(float(BLK))):
        angles = positions[:, None] * freqs[None, :]
        cosine, sine = np.cos(angles), np.sin(angles)
        joined = [np.concatenate([cosine, cosine], 1), np.concatenate([-sine, sine], 1)]
        out.append(jnp.asarray(np.stack(joined), jnp.float32))
    return out


def per_device(tokens, w_query, w_key, w_value, block_order):
    anywhere, vmem = pl.BlockSpec(memory_space=pl.ANY), pl.BlockSpec(memory_space=pltpu.VMEM)
    count = len(MESSAGES)
    return pl.pallas_call(
        kernel,
        out_shape=jax.ShapeDtypeStruct((256, 1024), jnp.bfloat16),
        in_specs=[anywhere] * 4 + [pl.BlockSpec(memory_space=pltpu.SMEM), vmem, vmem],
        out_specs=vmem,
        scratch_shapes=[
            pltpu.VMEM((2, 128, 4096), jnp.bfloat16),
            pltpu.VMEM((4096, 1024), jnp.bfloat16),
            pltpu.VMEM((4096, 256), jnp.bfloat16),
            pltpu.VMEM((2048, HD), jnp.bfloat16),
            pltpu.VMEM((CHUNKS, 2, ROWS, HD), jnp.bfloat16),
            pltpu.VMEM((CHUNKS, ROWS // HALF, 16, HD), jnp.bfloat16),
            pltpu.VMEM((2048, HD), jnp.float32),
            pltpu.VMEM((2048, 2 * HD), jnp.float32),
            pltpu.SemaphoreType.DMA((count,)),
            pltpu.SemaphoreType.DMA((count,)),
            pltpu.SemaphoreType.DMA((10,)),
            pltpu.SemaphoreType.DMA((8,)),
            pltpu.SemaphoreType.DMA((7,)),
        ],
        compiler_params=pltpu.CompilerParams(
            collective_id=0, has_side_effects=True, vmem_limit_bytes=56 << 20
        ),
        cost_estimate=pl.CostEstimate(flops=38 * 10**9, bytes_accessed=12 * 10**6, transcendentals=33 * 10**6),
    )(tokens, w_query, w_key, w_value, block_order, *rotary_tables())


def solution(mesh):
    return jax.shard_map(
        per_device,
        mesh=mesh,
        in_specs=(P(("ctx", "head"), None), P(None, "head"), P(None, "head"), P(None, "head"), P()),
        out_specs=P("ctx", "head"),
        check_vma=False,
    )
```

```python
import math

import jax
import jax.numpy as jnp
import numpy as np
from jax import lax
from jax.experimental import pallas as pl
from jax.experimental.pallas import tpu as pltpu
from jax.sharding import PartitionSpec as P

HD = 128
BLK = 128
NX, NY, NZ = 2, 4, 8
CHUNKS = 16
ROWS = 1024
HALF = 64
TILE = 512
WIDE = 256
AHEAD = 0
LOW = -1e30
FACTOR = math.log2(math.e) / math.sqrt(HD)
CONTRACT_LAST = (((1,), (1,)), ((), ()))
MOVES = {
    "x": (1, 0, 0), "y+": (0, 1, 0), "y-": (0, -1, 0), "z+": (0, 0, 1), "z-": (0, 0, -1),
    "y2": (0, 2, 0), "z+2": (0, 0, 2), "z-2": (0, 0, -2),
}
LOADS = {"y2": {"y+": 1, "y-": 1}, "z+2": {"z+": 2}, "z-2": {"z-": 2}}
KINDS = {"E": ("E1", "E2"), "L": ("L1", "L2")}
YS = (0, 1, 3, 2)
ZS = (0, 1, 7, 2, 6, 3, 5, 4)
BACKLOG = 3.0
PATHS = {"E1": "xzy", "E2": "yzx", "L1": "xzy", "L2": "xyz"}
FAR = ("E1", "E2", "L1", "L2",)
FIRST = [
    ("E2", "x"), ("L2", "y"), ("L2", "x"), ("E1", "y"), ("L1", "x"), ("E1", "x"),
    ("L2", "z"), ("L1", "z"), ("E2", "z"), ("E2", "y"), ("L1", "y"), ("E1", "z"),
]


def moved(item, way):
    kind, x, y, z = item
    dx, dy, dz = MOVES[way]
    return (kind, (x + dx) % NX, (y + dy) % NY, (z + dz) % NZ)


def run(kind, xs, ys, zs):
    return [(kind, x, y, z) for y in ys for z in zs for x in xs]


def all_groups():
    out = []
    for kind, path in PATHS.items():
        sides = [(0, 1)] if path[0] == "x" else [(0,), (1,)]
        for xs in sides:
            if path.index("y") < path.index("z"):
                for z in range(NZ):
                    out += [run(kind, xs, ys, (z,)) for ys in (YS[:2], YS[2:])]
            else:
                for y in range(NY):
                    out += [run(kind, xs, (y,), ZS[n : n + 2]) for n in (0, 2, 4, 6)]
    return out


def first_y(kind, xs, far):
    out = [(way, run(kind, (x,), (0,), (0,))) for x in xs for way in ("y+", "y-")]
    if far:
        return out + [("y2", run(kind, (x,), (0,), (0,))) for x in xs]
    out.append(("y+", run(kind, (0,), (1,), (0,))))
    return out + ([("y-", run(kind, (1,), (3,), (0,)))] if len(xs) > 1 else [])


def first_z(kind, xs, far):
    out = [(way, run(kind, (x,), (0,), (0,))) for x in xs for way in ("z+", "z-")]
    if far:
        out += [(way, run(kind, (x,), (0,), (0,))) for x in xs for way in ("z+2", "z-2")]
        out += [("z+", run(kind, xs, (0,), (2,))), ("z-", run(kind, xs, (0,), (6,)))]
        out.append(("z+2", run(kind, (0,), (0,), (2,))))
        return out + ([("z-2", run(kind, (1,), (0,), (6,)))] if len(xs) > 1 else [])
    for up, down in ((1, 7), (2, 6)):
        out += [("z+", run(kind, xs, (0,), (up,))), ("z-", run(kind, xs, (0,), (down,)))]
    out.append(("z+", run(kind, (0,), (0,), (3,))))
    return out + ([("z-", run(kind, (1,), (0,), (5,)))] if len(xs) > 1 else [])


def along_z(kind, xs):
    out = []
    for up, down in ((0, 0), (1, 7), (2, 6)):
        for ys in (YS[:1], YS[1:2], YS[2:]):
            out += [("z+", run(kind, xs, ys, (up,))), ("z-", run(kind, xs, ys, (down,)))]
    out.append(("z+", run(kind, xs, YS[:2], (3,))))
    return out + [("z-", run(kind, xs, YS[2:], (5,)))]


def along_y(kind, xs):
    out = []
    for zs in (ZS[:1], ZS[1:2], ZS[2:4], ZS[4:6], ZS[6:]):
        out += [(way, run(kind, xs, (0,), zs)) for way in ("y+", "y-")]
    for zs in (ZS[:2], ZS[2:4]):
        out.append(("y+", run(kind, xs, (1,), zs)))
    for zs in (ZS[4:6], ZS[6:]):
        out.append(("y-", run(kind, xs, (3,), zs)))
    return out


def stages(kind):
    path, both = PATHS[kind], (0, 1)
    xs = both if path[0] == "x" else (0,)
    if path.index("y") < path.index("z"):
        first, then = ("y", first_y(kind, xs, kind in FAR)), ("z", along_z(kind, xs))
        rows = [run(kind, (0,), ys, (z,)) for z in ZS for ys in (YS[:2], YS[2:])]
    else:
        first, then = ("z", first_z(kind, xs, kind in FAR)), ("y", along_y(kind, xs))
        rows = [run(kind, (0,), (y,), ZS[n : n + 2]) for y in YS for n in (0, 2, 4, 6)]
    if path[0] == "x":
        rows = [run(kind, (0,), (0,), (0,))]
    return dict([first, then, ("x", [("x", items) for items in rows])])


def all_messages():
    return [message for kind, axis in FIRST for message in stages(kind)[axis]]


def plan():
    messages, groups = all_messages(), all_groups()
    half_us, latency, issue_us, margin = 0.82, 2.8, 0.02, 0.4
    segments = [("qE", 0.6)] * 4 + [("ownE", 0.4)] + [("part", 0.8)] * 3 + [("ahead", 1.4)] * AHEAD
    segments += [("kvL", 0.5), ("qL", 1.2), ("ownL", 0.4)]
    segments += [("step", 2.75)] * (CHUNKS - AHEAD)
    tokens_at = [16.0, 12.5, 9.5, 6.5]
    have = {("E1", 0, 0, 0), ("E2", 0, 0, 0)}
    free = {way: 0.0 for way in MOVES if way not in LOADS}
    arrival, unsent, arrived, left = {}, list(range(len(messages))), set(), list(range(len(groups)))
    complete = {}
    now = 2.5
    actions, order = [], []

    def send_ready(acts):
        nonlocal now
        for m in list(unsent):
            way, items = messages[m]
            loads = LOADS.get(way, {way: 1})
            start = max(free[link] for link in loads)
            if start <= now + BACKLOG and all(item in have for item in items):
                unsent.remove(m)
                now += issue_us
                start = max(now, start)
                for link, load in loads.items():
                    free[link] = start + half_us * len(items) * load
                arrival[m] = max(free[link] for link in loads) + latency + (0.7 if way in LOADS else 0.0)
                acts.append(("send", m))

    def note():
        for g in left:
            if g not in complete and all(item in have for item in groups[g]):
                complete[g] = len(complete)

    def take(m, acts):
        nonlocal now
        acts.append(("wait", m))
        now = max(now, arrival[m]) + issue_us
        arrived.add(m)
        have.update(moved(item, messages[m][0]) for item in messages[m][1])
        note()
        send_ready(acts)

    def pending():
        return sorted((arrival[m], m) for m in arrival if m not in arrived)

    def choose(ready, room):
        if room == 0:
            return []
        for n, g in enumerate(ready):
            if len(groups[g]) <= room:
                rest = choose(ready[n + 1 :], room - len(groups[g]))
                if rest is not None:
                    return [g] + rest
        return None

    def chosen_now():
        ready = sorted((g for g in left if g in complete), key=complete.get)
        return choose(ready, ROWS // HALF) if sum(len(groups[g]) for g in ready) >= ROWS // HALF else None

    for what, length in segments:
        acts = []
        if what in ("part", "kvL"):
            now = max(now, tokens_at.pop())
        send_ready(acts)
        if not actions:
            free["x"] += 9.0
        while True:
            soon = [(t, m) for t, m in pending() if t <= now - margin]
            if not soon:
                break
            take(soon[0][1], acts)
        if what in ("step", "ahead"):
            while (chosen := chosen_now()) is None:
                take(pending()[0][1], acts)
            for g in chosen:
                left.remove(g)
            order.append(chosen)
        actions.append((what, acts))
        now += length
        if what == "kvL":
            have.update([("L1", 0, 0, 0), ("L2", 0, 0, 0)])
    assert not left and len(arrived) == len(messages)
    place = {}
    for chunk, chosen in enumerate(order):
        row = 0
        for g in chosen:
            for item in groups[g]:
                place[item] = (chunk, row)
                row += HALF
        assert row == ROWS
    return messages, actions, place, now


MESSAGES, ACTIONS, PLACE, ESTIMATE = plan()


def kernel(
    tok_in, wq_in, wk_in, wv_in, blocks, base, offset, out,
    tok, wq, wkv, query, kv, aug, largest, acc, late,
    send, recv, tok_sem, relay_sem, local,
):
    ctx, head = lax.axis_index("ctx"), lax.axis_index("head")
    x, y, z = ctx // 32, (ctx // 8) % 4, ctx % 8
    early, core = head // 2, head % 2

    def device(x, y, z):
        return ((x * 4 + y) * 8 + z, head)

    near = {
        "x": device(1 - x, y, z),
        "y+": device(x, (y + 1) % 4, z),
        "y-": device(x, (y + 3) % 4, z),
        "z+": device(x, y, (z + 1) % 8),
        "z-": device(x, y, (z + 7) % 8),
        "y2": device(x, (y + 2) % 4, z),
        "z+2": device(x, y, (z + 2) % 8),
        "z-2": device(x, y, (z + 6) % 8),
    }
    beside = (ctx, head + 1 - 2 * core)
    across = (ctx, (head + 2) % 4)

    barrier = pltpu.get_barrier_semaphore()
    peers = list(near.values()) + [beside, across]
    for peer in peers:
        pl.semaphore_signal(barrier, inc=1, device_id=peer, device_id_type=pl.DeviceIdType.MESH)

    mine = pl.ds(pl.multiple_of(core * 64, 64), 64)
    own_tokens = pltpu.make_async_copy(tok_in, tok.at[0, mine], local.at[2])
    own_tokens.start()
    copies = [
        pltpu.make_async_copy(wk_in, wkv.at[:, 0:HD], local.at[0]),
        pltpu.make_async_copy(wv_in, wkv.at[:, HD : 2 * HD], local.at[1]),
    ]
    for copy in copies:
        copy.start()
    wide = []
    for j in range(4):
        columns = pl.ds(j * WIDE, WIDE)
        wide.append(pltpu.make_async_copy(wq_in.at[:, columns], wq.at[:, columns], local.at[3 + j]))
        wide[-1].start()
    pl.semaphore_wait(barrier, len(peers))

    def remote(src, dst, s, r, to):
        return pltpu.make_async_remote_copy(
            src_ref=src, dst_ref=dst, send_sem=s, recv_sem=r, device_id=to,
            device_id_type=pl.DeviceIdType.MESH,
        )

    to_beside = remote(tok_in, tok.at[0, mine], tok_sem.at[0], tok_sem.at[1], beside)
    to_beside.start()
    to_across, relays = [], []
    for j in range(4):
        piece = pl.ds(j * ROWS, ROWS)
        to_across.append(
            remote(tok_in.at[:, piece], tok.at[1, mine, piece], tok_sem.at[2 + j], tok_sem.at[6 + j], across)
        )
        relays.append(
            remote(tok.at[1, mine, piece], tok.at[1, mine, piece], relay_sem.at[j], relay_sem.at[4 + j], beside)
        )
    to_across[0].start()

    own = [blocks[ctx * 2 + early], blocks[ctx * 2 + 1 - early]]
    lanes = lax.broadcasted_iota(jnp.int32, (16, HD), 1)
    bound = jnp.where(lanes == 0, own[0], jnp.where(lanes == 1, own[1], 1 << 20))
    for dx in range(NX):
        for dy in range(NY):
            for dz in range(NZ):
                origin = (((x + dx) % NX) * 4 + (y - dy + NY) % NY) * 8 + (z - dz + NZ) % NZ
                for part, kinds in ((early, KINDS["E"]), (1 - early, KINDS["L"])):
                    place = blocks[origin * 2 + part]
                    mask = jnp.where(place < bound, 0.0, LOW).astype(jnp.bfloat16)
                    for kind in kinds:
                        chunk, row = PLACE[(kind, dx, dy, dz)]
                        aug[chunk, row // HALF] = mask

    def slot(items):
        chunk, row = PLACE[items[0]]
        count = len(items) * HALF
        spots = [PLACE[item] for item in items]
        assert spots == [(chunk, row + n * HALF) for n in range(len(items))]
        return kv.at[chunk, :, pl.ds(row, count)]

    def message(m):
        way, items = MESSAGES[m]
        landing = [moved(item, way) for item in items]
        return remote(slot(items), slot(landing), send.at[m], recv.at[m], near[way])

    def communicate(acts):
        for what, m in acts:
            if what == "send":
                message(m).start()
            else:
                message(m).wait_recv()

    def rotation(part):
        turn = own[part]
        base_cos, base_sin = base[0, pl.ds(turn, 1)], base[1, pl.ds(turn, 1)]
        cosine = base_cos * offset[0] - base_sin * offset[1]
        sine = base_sin * offset[0] + base_cos * offset[1]
        return lambda values: (values * cosine + pltpu.roll(values, HD // 2, 1) * sine).astype(jnp.bfloat16)

    spots = [[(kind, 0, 0, 0) for kind in KINDS[part]] for part in "EL"]

    def store_kv(part, both):
        keys, values = rotation(part)(both[:, :HD]), both[:, HD:].astype(jnp.bfloat16)
        size = BLK // len(spots[part])
        for n, item in enumerate(spots[part]):
            chunk, row = PLACE[item]
            kv[chunk, 0, pl.ds(row, size)] = keys[n * size : (n + 1) * size]
            kv[chunk, 1, pl.ds(row, size)] = values[n * size : (n + 1) * size]

    def store_q(part, j, both):
        rotate = rotation(part)
        for h in range(2):
            rows = pl.ds(part * ROWS + (2 * j + h) * BLK, BLK)
            query[rows] = rotate(both[:, h * HD : (h + 1) * HD])

    def late_part(k, js):
        piece = pl.ds(k * ROWS, ROWS)
        for j in js:
            weights = wkv[piece] if j == 4 else wq[piece, j * WIDE : (j + 1) * WIDE]
            product = jnp.dot(tok[1, :, piece], weights, preferred_element_type=jnp.float32)
            if k:
                product = late[j] + product
            if k < 3:
                late[j] = product
            elif j == 4:
                store_kv(1, product)
            else:
                store_q(1, j, product)

    lane = lax.broadcasted_iota(jnp.int32, (TILE, HD), 1)
    marks = [jnp.where(lane == part, 1.0, 0.0).astype(jnp.bfloat16) for part in range(2)]

    def own_block(part):
        ones = jnp.ones((BLK, HD), jnp.bfloat16)
        row = lax.broadcasted_iota(jnp.int32, (TILE, BLK), 0) % BLK
        keep = lax.broadcasted_iota(jnp.int32, (TILE, BLK), 1) <= row
        size = BLK // len(spots[part])
        at = [PLACE[item] for item in spots[part]]
        keys, values = (
            jnp.concatenate([kv[chunk, n, pl.ds(row, size)] for chunk, row in at], 0) for n in range(2)
        )
        values = jnp.concatenate([values, ones], 1)
        for t in range(ROWS // TILE):
            rows = pl.ds(part * ROWS + t * TILE, TILE)
            scores = lax.dot_general(query[rows], keys, CONTRACT_LAST, preferred_element_type=jnp.float32)
            scores = jnp.where(keep, scores, LOW)
            top = jnp.broadcast_to(jnp.max(scores, axis=1, keepdims=True), (TILE, HD))
            expo = jnp.exp2((scores - top) * FACTOR).astype(jnp.bfloat16)
            largest[rows] = top
            acc[rows] = jnp.dot(expo, values, preferred_element_type=jnp.float32)

    def score(part, rows, chunk):
        masks = [aug[chunk, b] for b in range(ROWS // HALF) for _ in range(HALF // 16)]
        keys = jnp.concatenate([kv[chunk, 0], jnp.concatenate(masks, 0)], 1)
        wide_query = jnp.concatenate([query[rows], marks[part]], 1)
        return lax.dot_general(wide_query, keys, CONTRACT_LAST, preferred_element_type=jnp.float32)

    def weigh(rows, scores):
        before = largest[rows]
        after = jnp.maximum(before, jnp.max(scores, axis=1, keepdims=True))
        largest[rows] = after
        expo = [
            jnp.exp2((scores[:, n : n + HD] - after) * FACTOR).astype(jnp.bfloat16) for n in range(0, ROWS, HD)
        ]
        return jnp.concatenate(expo, 1), jnp.exp2((before - after) * FACTOR)

    def gather(rows, chunk, expo, shrink):
        values = jnp.concatenate([kv[chunk, 1], jnp.ones((ROWS, HD), jnp.bfloat16)], 1)
        product = jnp.dot(expo, values, preferred_element_type=jnp.float32)
        acc[rows] = acc[rows] * jnp.concatenate([shrink, shrink], 1) + product

    def attend(pairs):
        work = [
            (part, pl.ds(part * ROWS + t * TILE, TILE), chunk) for part, chunk in pairs for t in range(ROWS // TILE)
        ]
        scores, weights = {}, {}
        for n in range(len(work) + 2):
            if n < len(work):
                scores[n] = score(*work[n])
            if n >= 2:
                part, rows, chunk = work[n - 2]
                gather(rows, chunk, *weights.pop(n - 2))
            if 1 <= n <= len(work):
                weights[n - 1] = weigh(work[n - 1][1], scores.pop(n - 1))

    own_tokens.wait()
    to_beside.wait_recv()
    for copy in copies:
        copy.wait()
    store_kv(0, jnp.dot(tok[0], wkv[...], preferred_element_type=jnp.float32))
    step_acts = []
    count = {what: 0 for what, _ in ACTIONS}
    for what, acts in ACTIONS:
        n = count[what]
        count[what] += 1
        if what == "step":
            step_acts.append(acts)
            continue
        communicate(acts)
        if what == "qE" and n == 0:
            for k in range(1, 4):
                to_across[k].start()
        if what == "qE":
            wide[n].wait()
            columns = slice(n * WIDE, (n + 1) * WIDE)
            store_q(0, n, jnp.dot(tok[0], wq[:, columns], preferred_element_type=jnp.float32))
        elif what == "ownE":
            own_block(0)
        elif what == "ahead":
            attend([(0, n)])
        elif what == "part":
            to_across[n].wait_recv()
            relays[n].start()
            if n:
                relays[n - 1].wait_recv()
                late_part(n - 1, range(5))
        elif what == "kvL":
            to_across[3].wait_recv()
            relays[3].start()
            relays[2].wait_recv()
            late_part(2, range(5))
            relays[3].wait_recv()
            late_part(3, [4])
        elif what == "qL":
            late_part(3, range(4))
        else:
            own_block(1)

    def one_step(step, carry):
        for s, acts in enumerate(step_acts):
            if acts:

                @pl.when(step == s)
                def _(acts=acts):
                    communicate(acts)

        attend([(1, step), (0, step + AHEAD)])
        return carry

    lax.fori_loop(0, CHUNKS - AHEAD, one_step, 0)
    attend([(1, chunk) for chunk in range(CHUNKS - AHEAD, CHUNKS)])

    for part in range(2):
        block = pl.ds(pl.multiple_of((early if part == 0 else 1 - early) * BLK, BLK), BLK)
        for h in range(8):
            rows = pl.ds(part * ROWS + h * BLK, BLK)
            total = acc[rows]
            out[block, h * HD : (h + 1) * HD] = (total[:, :HD] / total[:, HD:]).astype(jnp.bfloat16)

    for m in range(len(MESSAGES)):
        message(m).wait_send()
    to_beside.wait_send()
    for k in range(4):
        to_across[k].wait_send()
        relays[k].wait_send()


def rotary_tables():
    freqs = 500000.0 ** (-(np.arange(HD // 2) * 2.0) / HD)
    out = []
    for positions in (np.arange(128.0) * BLK, np.arange(float(BLK))):
        angles = positions[:, None] * freqs[None, :]
        cosine, sine = np.cos(angles), np.sin(angles)
        joined = [np.concatenate([cosine, cosine], 1), np.concatenate([-sine, sine], 1)]
        out.append(jnp.asarray(np.stack(joined), jnp.float32))
    return out


def per_device(tokens, w_query, w_key, w_value, block_order):
    anywhere, vmem = pl.BlockSpec(memory_space=pl.ANY), pl.BlockSpec(memory_space=pltpu.VMEM)
    count = len(MESSAGES)
    return pl.pallas_call(
        kernel,
        out_shape=jax.ShapeDtypeStruct((256, 1024), jnp.bfloat16),
        in_specs=[anywhere] * 4 + [pl.BlockSpec(memory_space=pltpu.SMEM), vmem, vmem],
        out_specs=vmem,
        scratch_shapes=[
            pltpu.VMEM((2, 128, 4096), jnp.bfloat16),
            pltpu.VMEM((4096, 1024), jnp.bfloat16),
            pltpu.VMEM((4096, 256), jnp.bfloat16),
            pltpu.VMEM((2048, HD), jnp.bfloat16),
            pltpu.VMEM((CHUNKS, 2, ROWS, HD), jnp.bfloat16),
            pltpu.VMEM((CHUNKS, ROWS // HALF, 16, HD), jnp.bfloat16),
            pltpu.VMEM((2048, HD), jnp.float32),
            pltpu.VMEM((2048, 2 * HD), jnp.float32),
            pltpu.VMEM((5, BLK, WIDE), jnp.float32),
            pltpu.SemaphoreType.DMA((count,)),
            pltpu.SemaphoreType.DMA((count,)),
            pltpu.SemaphoreType.DMA((10,)),
            pltpu.SemaphoreType.DMA((8,)),
            pltpu.SemaphoreType.DMA((7,)),
        ],
        compiler_params=pltpu.CompilerParams(
            collective_id=0, has_side_effects=True, vmem_limit_bytes=56 << 20
        ),
        cost_estimate=pl.CostEstimate(flops=38 * 10**9, bytes_accessed=12 * 10**6, transcendentals=33 * 10**6),
    )(tokens, w_query, w_key, w_value, block_order, *rotary_tables())


def solution(mesh):
    return jax.shard_map(
        per_device,
        mesh=mesh,
        in_specs=(P(("ctx", "head"), None), P(None, "head"), P(None, "head"), P(None, "head"), P()),
        out_specs=P("ctx", "head"),
        check_vma=False,
    )
```

```python
import math

import jax
import jax.numpy as jnp
import numpy as np
from jax import lax
from jax.experimental import pallas as pl
from jax.experimental.pallas import tpu as pltpu
from jax.sharding import PartitionSpec as P

HD = 128
BLK = 128
NX, NY, NZ = 2, 4, 8
CHUNKS = 16
ROWS = 1024
HALF = 64
TILE = 512
WIDE = 256
AHEAD = 0
LOW = -1e30
FACTOR = math.log2(math.e) / math.sqrt(HD)
CONTRACT_LAST = (((1,), (1,)), ((), ()))
MOVES = {
    "x": (1, 0, 0), "y+": (0, 1, 0), "y-": (0, -1, 0), "z+": (0, 0, 1), "z-": (0, 0, -1),
    "y2": (0, 2, 0), "z+2": (0, 0, 2), "z-2": (0, 0, -2),
}
LOADS = {"y2": {"y+": 1, "y-": 1}, "z+2": {"z+": 2}, "z-2": {"z-": 2}}
KINDS = {"E": ("E1", "E2"), "L": ("L1", "L2")}
YS = (0, 1, 3, 2)
ZS = (0, 1, 7, 2, 6, 3, 5, 4)
BACKLOG = 3.0
PATHS = {"E1": "xzy", "E2": "yzx", "L1": "xzy", "L2": "xyz"}
FAR = ("E1", "E2", "L1", "L2",)
FIRST = [
    ("E2", "x"), ("L2", "y"), ("L2", "x"), ("E1", "y"), ("L1", "x"), ("E1", "x"),
    ("L2", "z"), ("L1", "z"), ("E2", "z"), ("E2", "y"), ("L1", "y"), ("E1", "z"),
]


def moved(item, way):
    kind, x, y, z = item
    dx, dy, dz = MOVES[way]
    return (kind, (x + dx) % NX, (y + dy) % NY, (z + dz) % NZ)


def run(kind, xs, ys, zs):
    return [(kind, x, y, z) for y in ys for z in zs for x in xs]


def all_groups():
    out = []
    for kind, path in PATHS.items():
        sides = [(0, 1)] if path[0] == "x" else [(0,), (1,)]
        for xs in sides:
            if path.index("y") < path.index("z"):
                for z in range(NZ):
                    out += [run(kind, xs, ys, (z,)) for ys in (YS[:2], YS[2:])]
            else:
                for y in range(NY):
                    out += [run(kind, xs, (y,), ZS[n : n + 2]) for n in (0, 2, 4, 6)]
    return out


def first_y(kind, xs, far):
    out = [(way, run(kind, (x,), (0,), (0,))) for x in xs for way in ("y+", "y-")]
    if far:
        return out + [("y2", run(kind, (x,), (0,), (0,))) for x in xs]
    out.append(("y+", run(kind, (0,), (1,), (0,))))
    return out + ([("y-", run(kind, (1,), (3,), (0,)))] if len(xs) > 1 else [])


def first_z(kind, xs, far):
    out = [(way, run(kind, (x,), (0,), (0,))) for x in xs for way in ("z+", "z-")]
    if far:
        out += [(way, run(kind, (x,), (0,), (0,))) for x in xs for way in ("z+2", "z-2")]
        out += [("z+", run(kind, xs, (0,), (2,))), ("z-", run(kind, xs, (0,), (6,)))]
        out.append(("z+2", run(kind, (0,), (0,), (2,))))
        return out + ([("z-2", run(kind, (1,), (0,), (6,)))] if len(xs) > 1 else [])
    for up, down in ((1, 7), (2, 6)):
        out += [("z+", run(kind, xs, (0,), (up,))), ("z-", run(kind, xs, (0,), (down,)))]
    out.append(("z+", run(kind, (0,), (0,), (3,))))
    return out + ([("z-", run(kind, (1,), (0,), (5,)))] if len(xs) > 1 else [])


def along_z(kind, xs):
    out = []
    for up, down in ((0, 0), (1, 7), (2, 6)):
        for ys in (YS[:1], YS[1:2], YS[2:]):
            out += [("z+", run(kind, xs, ys, (up,))), ("z-", run(kind, xs, ys, (down,)))]
    out.append(("z+", run(kind, xs, YS[:2], (3,))))
    return out + [("z-", run(kind, xs, YS[2:], (5,)))]


def along_y(kind, xs):
    out = []
    for zs in (ZS[:1], ZS[1:2], ZS[2:4], ZS[4:6], ZS[6:]):
        out += [(way, run(kind, xs, (0,), zs)) for way in ("y+", "y-")]
    for zs in (ZS[:2], ZS[2:4]):
        out.append(("y+", run(kind, xs, (1,), zs)))
    for zs in (ZS[4:6], ZS[6:]):
        out.append(("y-", run(kind, xs, (3,), zs)))
    return out


def stages(kind):
    path, both = PATHS[kind], (0, 1)
    xs = both if path[0] == "x" else (0,)
    if path.index("y") < path.index("z"):
        first, then = ("y", first_y(kind, xs, kind in FAR)), ("z", along_z(kind, xs))
        rows = [run(kind, (0,), ys, (z,)) for z in ZS for ys in (YS[:2], YS[2:])]
    else:
        first, then = ("z", first_z(kind, xs, kind in FAR)), ("y", along_y(kind, xs))
        rows = [run(kind, (0,), (y,), ZS[n : n + 2]) for y in YS for n in (0, 2, 4, 6)]
    if path[0] == "x":
        rows = [run(kind, (0,), (0,), (0,))]
    return dict([first, then, ("x", [("x", items) for items in rows])])


def all_messages():
    return [message for kind, axis in FIRST for message in stages(kind)[axis]]


def plan():
    messages, groups = all_messages(), all_groups()
    half_us, latency, issue_us, margin = 0.82, 2.8, 0.02, 0.4
    segments = [("qE", 0.6)] * 4 + [("ownE", 0.4)] + [("part", 0.8)] * 3 + [("ahead", 1.4)] * AHEAD
    segments += [("kvL", 0.5), ("qL", 1.2), ("ownL", 0.4)]
    segments += [("step", 2.75)] * (CHUNKS - AHEAD)
    tokens_at = [16.0, 12.5, 9.5, 6.5]
    have = {("E1", 0, 0, 0), ("E2", 0, 0, 0)}
    free = {way: 0.0 for way in MOVES if way not in LOADS}
    arrival, unsent, arrived, left = {}, list(range(len(messages))), set(), list(range(len(groups)))
    complete = {}
    now = 2.5
    actions, order = [], []

    def send_ready(acts):
        nonlocal now
        for m in list(unsent):
            way, items = messages[m]
            loads = LOADS.get(way, {way: 1})
            start = max(free[link] for link in loads)
            if start <= now + BACKLOG and all(item in have for item in items):
                unsent.remove(m)
                now += issue_us
                start = max(now, start)
                for link, load in loads.items():
                    free[link] = start + half_us * len(items) * load
                arrival[m] = max(free[link] for link in loads) + latency + (0.7 if way in LOADS else 0.0)
                acts.append(("send", m))

    def note():
        for g in left:
            if g not in complete and all(item in have for item in groups[g]):
                complete[g] = len(complete)

    def take(m, acts):
        nonlocal now
        acts.append(("wait", m))
        now = max(now, arrival[m]) + issue_us
        arrived.add(m)
        have.update(moved(item, messages[m][0]) for item in messages[m][1])
        note()
        send_ready(acts)

    def pending():
        return sorted((arrival[m], m) for m in arrival if m not in arrived)

    def choose(ready, room):
        if room == 0:
            return []
        for n, g in enumerate(ready):
            if len(groups[g]) <= room:
                rest = choose(ready[n + 1 :], room - len(groups[g]))
                if rest is not None:
                    return [g] + rest
        return None

    def chosen_now():
        ready = sorted((g for g in left if g in complete), key=complete.get)
        return choose(ready, ROWS // HALF) if sum(len(groups[g]) for g in ready) >= ROWS // HALF else None

    for what, length in segments:
        acts = []
        if what in ("part", "kvL"):
            now = max(now, tokens_at.pop())
        send_ready(acts)
        if not actions:
            free["x"] += 9.0
        while True:
            soon = [(t, m) for t, m in pending() if t <= now - margin]
            if not soon:
                break
            take(soon[0][1], acts)
        if what in ("step", "ahead"):
            while (chosen := chosen_now()) is None:
                take(pending()[0][1], acts)
            for g in chosen:
                left.remove(g)
            order.append(chosen)
        actions.append((what, acts))
        now += length
        if what == "kvL":
            have.update([("L1", 0, 0, 0), ("L2", 0, 0, 0)])
    assert not left and len(arrived) == len(messages)
    place = {}
    for chunk, chosen in enumerate(order):
        row = 0
        for g in chosen:
            for item in groups[g]:
                place[item] = (chunk, row)
                row += HALF
        assert row == ROWS
    return messages, actions, place, now


MESSAGES, ACTIONS, PLACE, ESTIMATE = plan()


def kernel(
    tok_in, wq_in, wk_in, wv_in, blocks, base, offset, out,
    tok, wq, wkv, query, kv, aug, largest, acc, late,
    send, recv, tok_sem, relay_sem, local,
):
    ctx, head = lax.axis_index("ctx"), lax.axis_index("head")
    x, y, z = ctx // 32, (ctx // 8) % 4, ctx % 8
    early, core = head // 2, head % 2

    def device(x, y, z):
        return ((x * 4 + y) * 8 + z, head)

    near = {
        "x": device(1 - x, y, z),
        "y+": device(x, (y + 1) % 4, z),
        "y-": device(x, (y + 3) % 4, z),
        "z+": device(x, y, (z + 1) % 8),
        "z-": device(x, y, (z + 7) % 8),
        "y2": device(x, (y + 2) % 4, z),
        "z+2": device(x, y, (z + 2) % 8),
        "z-2": device(x, y, (z + 6) % 8),
    }
    beside = (ctx, head + 1 - 2 * core)
    across = (ctx, (head + 2) % 4)

    barrier = pltpu.get_barrier_semaphore()
    peers = list(near.values()) + [beside, across]
    for peer in peers:
        pl.semaphore_signal(barrier, inc=1, device_id=peer, device_id_type=pl.DeviceIdType.MESH)

    mine = pl.ds(pl.multiple_of(core * 64, 64), 64)
    own_tokens = pltpu.make_async_copy(tok_in, tok.at[0, mine], local.at[2])
    own_tokens.start()
    copies = [
        pltpu.make_async_copy(wk_in, wkv.at[:, 0:HD], local.at[0]),
        pltpu.make_async_copy(wv_in, wkv.at[:, HD : 2 * HD], local.at[1]),
    ]
    for copy in copies:
        copy.start()
    wide = []
    for j in range(4):
        columns = pl.ds(j * WIDE, WIDE)
        wide.append(pltpu.make_async_copy(wq_in.at[:, columns], wq.at[:, columns], local.at[3 + j]))
        wide[-1].start()
    pl.semaphore_wait(barrier, len(peers))

    def remote(src, dst, s, r, to):
        return pltpu.make_async_remote_copy(
            src_ref=src, dst_ref=dst, send_sem=s, recv_sem=r, device_id=to,
            device_id_type=pl.DeviceIdType.MESH,
        )

    to_beside = remote(tok_in, tok.at[0, mine], tok_sem.at[0], tok_sem.at[1], beside)
    to_beside.start()
    to_across, relays = [], []
    for j in range(4):
        piece = pl.ds(j * ROWS, ROWS)
        to_across.append(
            remote(tok_in.at[:, piece], tok.at[1, mine, piece], tok_sem.at[2 + j], tok_sem.at[6 + j], across)
        )
        relays.append(
            remote(tok.at[1, mine, piece], tok.at[1, mine, piece], relay_sem.at[j], relay_sem.at[4 + j], beside)
        )
    to_across[0].start()

    own = [blocks[ctx * 2 + early], blocks[ctx * 2 + 1 - early]]

    def mask_blocks():
        lanes = lax.broadcasted_iota(jnp.int32, (16, HD), 1)
        bound = jnp.where(lanes == 0, own[0], jnp.where(lanes == 1, own[1], 1 << 20))
        for dx in range(NX):
            for dy in range(NY):
                for dz in range(NZ):
                    origin = (((x + dx) % NX) * 4 + (y - dy + NY) % NY) * 8 + (z - dz + NZ) % NZ
                    for part, kinds in ((early, KINDS["E"]), (1 - early, KINDS["L"])):
                        place = blocks[origin * 2 + part]
                        mask = jnp.where(place < bound, 0.0, LOW).astype(jnp.bfloat16)
                        for kind in kinds:
                            chunk, row = PLACE[(kind, dx, dy, dz)]
                            aug[chunk, row // HALF] = mask

    def slot(items):
        chunk, row = PLACE[items[0]]
        count = len(items) * HALF
        spots = [PLACE[item] for item in items]
        assert spots == [(chunk, row + n * HALF) for n in range(len(items))]
        return kv.at[chunk, :, pl.ds(row, count)]

    def message(m):
        way, items = MESSAGES[m]
        landing = [moved(item, way) for item in items]
        return remote(slot(items), slot(landing), send.at[m], recv.at[m], near[way])

    def communicate(acts):
        for what, m in acts:
            if what == "send":
                message(m).start()
            else:
                message(m).wait_recv()

    def rotation(part):
        turn = own[part]
        base_cos, base_sin = base[0, pl.ds(turn, 1)], base[1, pl.ds(turn, 1)]
        cosine = base_cos * offset[0] - base_sin * offset[1]
        sine = base_sin * offset[0] + base_cos * offset[1]
        return lambda values: (values * cosine + pltpu.roll(values, HD // 2, 1) * sine).astype(jnp.bfloat16)

    spots = [[(kind, 0, 0, 0) for kind in KINDS[part]] for part in "EL"]

    def store_kv(part, both):
        keys, values = rotation(part)(both[:, :HD]), both[:, HD:].astype(jnp.bfloat16)
        size = BLK // len(spots[part])
        for n, item in enumerate(spots[part]):
            chunk, row = PLACE[item]
            kv[chunk, 0, pl.ds(row, size)] = keys[n * size : (n + 1) * size]
            kv[chunk, 1, pl.ds(row, size)] = values[n * size : (n + 1) * size]

    def store_q(part, j, both):
        rotate = rotation(part)
        for h in range(2):
            rows = pl.ds(part * ROWS + (2 * j + h) * BLK, BLK)
            query[rows] = rotate(both[:, h * HD : (h + 1) * HD])

    def late_part(k, js):
        piece = pl.ds(k * ROWS, ROWS)
        for j in js:
            weights = wkv[piece] if j == 4 else wq[piece, j * WIDE : (j + 1) * WIDE]
            product = jnp.dot(tok[1, :, piece], weights, preferred_element_type=jnp.float32)
            if k:
                product = late[j] + product
            if k < 3:
                late[j] = product
            elif j == 4:
                store_kv(1, product)
            else:
                store_q(1, j, product)

    lane = lax.broadcasted_iota(jnp.int32, (TILE, HD), 1)
    marks = [jnp.where(lane == part, 1.0, 0.0).astype(jnp.bfloat16) for part in range(2)]

    def own_block(part):
        ones = jnp.ones((BLK, HD), jnp.bfloat16)
        row = lax.broadcasted_iota(jnp.int32, (TILE, BLK), 0) % BLK
        keep = lax.broadcasted_iota(jnp.int32, (TILE, BLK), 1) <= row
        size = BLK // len(spots[part])
        at = [PLACE[item] for item in spots[part]]
        keys, values = (
            jnp.concatenate([kv[chunk, n, pl.ds(row, size)] for chunk, row in at], 0) for n in range(2)
        )
        values = jnp.concatenate([values, ones], 1)
        for t in range(ROWS // TILE):
            rows = pl.ds(part * ROWS + t * TILE, TILE)
            scores = lax.dot_general(query[rows], keys, CONTRACT_LAST, preferred_element_type=jnp.float32)
            scores = jnp.where(keep, scores, LOW)
            top = jnp.broadcast_to(jnp.max(scores, axis=1, keepdims=True), (TILE, HD))
            expo = jnp.exp2((scores - top) * FACTOR).astype(jnp.bfloat16)
            largest[rows] = top
            acc[rows] = jnp.dot(expo, values, preferred_element_type=jnp.float32)

    def score(part, rows, chunk):
        masks = [aug[chunk, b] for b in range(ROWS // HALF) for _ in range(HALF // 16)]
        keys = jnp.concatenate([kv[chunk, 0], jnp.concatenate(masks, 0)], 1)
        wide_query = jnp.concatenate([query[rows], marks[part]], 1)
        return lax.dot_general(wide_query, keys, CONTRACT_LAST, preferred_element_type=jnp.float32)

    def weigh(rows, scores):
        before = largest[rows]
        after = jnp.maximum(before, jnp.max(scores, axis=1, keepdims=True))
        largest[rows] = after
        expo = [
            jnp.exp2((scores[:, n : n + HD] - after) * FACTOR).astype(jnp.bfloat16) for n in range(0, ROWS, HD)
        ]
        return jnp.concatenate(expo, 1), jnp.exp2((before - after) * FACTOR)

    def gather(rows, chunk, expo, shrink):
        values = jnp.concatenate([kv[chunk, 1], jnp.ones((ROWS, HD), jnp.bfloat16)], 1)
        product = jnp.dot(expo, values, preferred_element_type=jnp.float32)
        acc[rows] = acc[rows] * jnp.concatenate([shrink, shrink], 1) + product

    def attend(pairs):
        work = [
            (part, pl.ds(part * ROWS + t * TILE, TILE), chunk) for part, chunk in pairs for t in range(ROWS // TILE)
        ]
        scores, weights = {}, {}
        for n in range(len(work) + 2):
            if n < len(work):
                scores[n] = score(*work[n])
            if n >= 2:
                part, rows, chunk = work[n - 2]
                gather(rows, chunk, *weights.pop(n - 2))
            if 1 <= n <= len(work):
                weights[n - 1] = weigh(work[n - 1][1], scores.pop(n - 1))

    own_tokens.wait()
    to_beside.wait_recv()
    for copy in copies:
        copy.wait()
    store_kv(0, jnp.dot(tok[0], wkv[...], preferred_element_type=jnp.float32))
    step_acts = []
    count = {what: 0 for what, _ in ACTIONS}
    for what, acts in ACTIONS:
        n = count[what]
        count[what] += 1
        if what == "step":
            step_acts.append(acts)
            continue
        communicate(acts)
        if what == "qE" and n == 0:
            for k in range(1, 4):
                to_across[k].start()
            mask_blocks()
        if what == "qE":
            wide[n].wait()
            columns = slice(n * WIDE, (n + 1) * WIDE)
            store_q(0, n, jnp.dot(tok[0], wq[:, columns], preferred_element_type=jnp.float32))
        elif what == "ownE":
            own_block(0)
        elif what == "ahead":
            attend([(0, n)])
        elif what == "part":
            to_across[n].wait_recv()
            relays[n].start()
            if n:
                relays[n - 1].wait_recv()
                late_part(n - 1, range(5))
        elif what == "kvL":
            to_across[3].wait_recv()
            relays[3].start()
            relays[2].wait_recv()
            late_part(2, range(5))
            relays[3].wait_recv()
            late_part(3, [4])
        elif what == "qL":
            late_part(3, range(4))
        else:
            own_block(1)

    def one_step(step, carry):
        def pick(low, high):
            if high - low == 1:
                communicate(step_acts[low])
            else:
                middle = (low + high) // 2
                pl.when(step < middle)(lambda: pick(low, middle))
                pl.when(step >= middle)(lambda: pick(middle, high))

        pick(0, len(step_acts))
        attend([(1, step), (0, step + AHEAD)])
        return carry

    lax.fori_loop(0, CHUNKS - AHEAD, one_step, 0)
    attend([(1, chunk) for chunk in range(CHUNKS - AHEAD, CHUNKS)])

    for part in range(2):
        block = pl.ds(pl.multiple_of((early if part == 0 else 1 - early) * BLK, BLK), BLK)
        for h in range(8):
            rows = pl.ds(part * ROWS + h * BLK, BLK)
            total = acc[rows]
            out[block, h * HD : (h + 1) * HD] = (total[:, :HD] / total[:, HD:]).astype(jnp.bfloat16)

    for m in range(len(MESSAGES)):
        message(m).wait_send()
    to_beside.wait_send()
    for k in range(4):
        to_across[k].wait_send()
        relays[k].wait_send()


def rotary_tables():
    freqs = 500000.0 ** (-(np.arange(HD // 2) * 2.0) / HD)
    out = []
    for positions in (np.arange(128.0) * BLK, np.arange(float(BLK))):
        angles = positions[:, None] * freqs[None, :]
        cosine, sine = np.cos(angles), np.sin(angles)
        joined = [np.concatenate([cosine, cosine], 1), np.concatenate([-sine, sine], 1)]
        out.append(jnp.asarray(np.stack(joined), jnp.float32))
    return out


def per_device(tokens, w_query, w_key, w_value, block_order):
    anywhere, vmem = pl.BlockSpec(memory_space=pl.ANY), pl.BlockSpec(memory_space=pltpu.VMEM)
    count = len(MESSAGES)
    return pl.pallas_call(
        kernel,
        out_shape=jax.ShapeDtypeStruct((256, 1024), jnp.bfloat16),
        in_specs=[anywhere] * 4 + [pl.BlockSpec(memory_space=pltpu.SMEM), vmem, vmem],
        out_specs=vmem,
        scratch_shapes=[
            pltpu.VMEM((2, 128, 4096), jnp.bfloat16),
            pltpu.VMEM((4096, 1024), jnp.bfloat16),
            pltpu.VMEM((4096, 256), jnp.bfloat16),
            pltpu.VMEM((2048, HD), jnp.bfloat16),
            pltpu.VMEM((CHUNKS, 2, ROWS, HD), jnp.bfloat16),
            pltpu.VMEM((CHUNKS, ROWS // HALF, 16, HD), jnp.bfloat16),
            pltpu.VMEM((2048, HD), jnp.float32),
            pltpu.VMEM((2048, 2 * HD), jnp.float32),
            pltpu.VMEM((5, BLK, WIDE), jnp.float32),
            pltpu.SemaphoreType.DMA((count,)),
            pltpu.SemaphoreType.DMA((count,)),
            pltpu.SemaphoreType.DMA((10,)),
            pltpu.SemaphoreType.DMA((8,)),
            pltpu.SemaphoreType.DMA((7,)),
        ],
        compiler_params=pltpu.CompilerParams(
            collective_id=0, has_side_effects=True, vmem_limit_bytes=56 << 20
        ),
        cost_estimate=pl.CostEstimate(flops=38 * 10**9, bytes_accessed=12 * 10**6, transcendentals=33 * 10**6),
    )(tokens, w_query, w_key, w_value, block_order, *rotary_tables())


def solution(mesh):
    return jax.shard_map(
        per_device,
        mesh=mesh,
        in_specs=(P(("ctx", "head"), None), P(None, "head"), P(None, "head"), P(None, "head"), P()),
        out_specs=P("ctx", "head"),
        check_vma=False,
    )
```

```python
import math

import jax
import jax.numpy as jnp
import numpy as np
from jax import lax
from jax.experimental import pallas as pl
from jax.experimental.pallas import tpu as pltpu
from jax.sharding import PartitionSpec as P

HD = 128
BLK = 128
NX, NY, NZ = 2, 4, 8
CHUNKS = 16
ROWS = 1024
HALF = 64
TILE = 512
WIDE = 256
AHEAD = 0
LOW = -1e30
FACTOR = math.log2(math.e) / math.sqrt(HD)
CONTRACT_LAST = (((1,), (1,)), ((), ()))
MOVES = {
    "x": (1, 0, 0), "y+": (0, 1, 0), "y-": (0, -1, 0), "z+": (0, 0, 1), "z-": (0, 0, -1),
    "y2": (0, 2, 0), "z+2": (0, 0, 2), "z-2": (0, 0, -2),
}
LOADS = {"y2": {"y+": 1, "y-": 1}, "z+2": {"z+": 2}, "z-2": {"z-": 2}}
KINDS = {"E": ("E1", "E2"), "L": ("L1", "L2")}
YS = (0, 1, 3, 2)
ZS = (0, 1, 7, 2, 6, 3, 5, 4)
BACKLOG = 3.0
PATHS = {"E1": "xzy", "E2": "yzx", "L1": "xzy", "L2": "xyz"}
FAR = ("E1", "E2", "L1", "L2",)
FIRST = [
    ("E2", "x"), ("L2", "y"), ("L2", "x"), ("E1", "y"), ("L1", "x"), ("E1", "x"),
    ("L2", "z"), ("L1", "z"), ("E2", "z"), ("E2", "y"), ("L1", "y"), ("E1", "z"),
]


def moved(item, way):
    kind, x, y, z = item
    dx, dy, dz = MOVES[way]
    return (kind, (x + dx) % NX, (y + dy) % NY, (z + dz) % NZ)


def run(kind, xs, ys, zs):
    return [(kind, x, y, z) for y in ys for z in zs for x in xs]


def all_groups():
    out = []
    for kind, path in PATHS.items():
        sides = [(0, 1)] if path[0] == "x" else [(0,), (1,)]
        for xs in sides:
            if path.index("y") < path.index("z"):
                for z in range(NZ):
                    out += [run(kind, xs, ys, (z,)) for ys in (YS[:2], YS[2:])]
            else:
                for y in range(NY):
                    out += [run(kind, xs, (y,), ZS[n : n + 2]) for n in (0, 2, 4, 6)]
    return out


def first_y(kind, xs, far):
    out = [(way, run(kind, (x,), (0,), (0,))) for x in xs for way in ("y+", "y-")]
    if far:
        return out + [("y2", run(kind, (x,), (0,), (0,))) for x in xs]
    out.append(("y+", run(kind, (0,), (1,), (0,))))
    return out + ([("y-", run(kind, (1,), (3,), (0,)))] if len(xs) > 1 else [])


def first_z(kind, xs, far):
    out = [(way, run(kind, (x,), (0,), (0,))) for x in xs for way in ("z+", "z-")]
    if far:
        out += [(way, run(kind, (x,), (0,), (0,))) for x in xs for way in ("z+2", "z-2")]
        out += [("z+", run(kind, xs, (0,), (2,))), ("z-", run(kind, xs, (0,), (6,)))]
        out.append(("z+2", run(kind, (0,), (0,), (2,))))
        return out + ([("z-2", run(kind, (1,), (0,), (6,)))] if len(xs) > 1 else [])
    for up, down in ((1, 7), (2, 6)):
        out += [("z+", run(kind, xs, (0,), (up,))), ("z-", run(kind, xs, (0,), (down,)))]
    out.append(("z+", run(kind, (0,), (0,), (3,))))
    return out + ([("z-", run(kind, (1,), (0,), (5,)))] if len(xs) > 1 else [])


def along_z(kind, xs):
    out = []
    for up, down in ((0, 0), (1, 7), (2, 6)):
        for ys in (YS[:1], YS[1:2], YS[2:]):
            out += [("z+", run(kind, xs, ys, (up,))), ("z-", run(kind, xs, ys, (down,)))]
    out.append(("z+", run(kind, xs, YS[:2], (3,))))
    return out + [("z-", run(kind, xs, YS[2:], (5,)))]


def along_y(kind, xs):
    out = []
    for zs in (ZS[:1], ZS[1:2], ZS[2:4], ZS[4:6], ZS[6:]):
        out += [(way, run(kind, xs, (0,), zs)) for way in ("y+", "y-")]
    for zs in (ZS[:2], ZS[2:4]):
        out.append(("y+", run(kind, xs, (1,), zs)))
    for zs in (ZS[4:6], ZS[6:]):
        out.append(("y-", run(kind, xs, (3,), zs)))
    return out


def stages(kind):
    path, both = PATHS[kind], (0, 1)
    xs = both if path[0] == "x" else (0,)
    if path.index("y") < path.index("z"):
        first, then = ("y", first_y(kind, xs, kind in FAR)), ("z", along_z(kind, xs))
        rows = [run(kind, (0,), ys, (z,)) for z in ZS for ys in (YS[:2], YS[2:])]
    else:
        first, then = ("z", first_z(kind, xs, kind in FAR)), ("y", along_y(kind, xs))
        rows = [run(kind, (0,), (y,), ZS[n : n + 2]) for y in YS for n in (0, 2, 4, 6)]
    if path[0] == "x":
        rows = [run(kind, (0,), (0,), (0,))]
    return dict([first, then, ("x", [("x", items) for items in rows])])


def all_messages():
    return [message for kind, axis in FIRST for message in stages(kind)[axis]]


def plan():
    messages, groups = all_messages(), all_groups()
    half_us, latency, issue_us, margin = 0.82, 2.8, 0.02, 0.4
    segments = [("qE", 0.6)] * 4 + [("ownE", 0.4)] + [("part", 0.8)] * 3 + [("ahead", 1.4)] * AHEAD
    segments += [("kvL", 0.5), ("qL", 1.2), ("ownL", 0.4)]
    segments += [("step", 2.75)] * (CHUNKS - AHEAD)
    tokens_at = [16.0, 12.5, 9.5, 6.5]
    have = {("E1", 0, 0, 0), ("E2", 0, 0, 0)}
    free = {way: 0.0 for way in MOVES if way not in LOADS}
    arrival, unsent, arrived, left = {}, list(range(len(messages))), set(), list(range(len(groups)))
    complete = {}
    now = 2.5
    actions, order = [], []

    def send_ready(acts):
        nonlocal now
        for m in list(unsent):
            way, items = messages[m]
            loads = LOADS.get(way, {way: 1})
            start = max(free[link] for link in loads)
            if start <= now + BACKLOG and all(item in have for item in items):
                unsent.remove(m)
                now += issue_us
                start = max(now, start)
                for link, load in loads.items():
                    free[link] = start + half_us * len(items) * load
                arrival[m] = max(free[link] for link in loads) + latency + (0.7 if way in LOADS else 0.0)
                acts.append(("send", m))

    def note():
        for g in left:
            if g not in complete and all(item in have for item in groups[g]):
                complete[g] = len(complete)

    def take(m, acts):
        nonlocal now
        acts.append(("wait", m))
        now = max(now, arrival[m]) + issue_us
        arrived.add(m)
        have.update(moved(item, messages[m][0]) for item in messages[m][1])
        note()
        send_ready(acts)

    def pending():
        return sorted((arrival[m], m) for m in arrival if m not in arrived)

    def choose(ready, room):
        if room == 0:
            return []
        for n, g in enumerate(ready):
            if len(groups[g]) <= room:
                rest = choose(ready[n + 1 :], room - len(groups[g]))
                if rest is not None:
                    return [g] + rest
        return None

    def chosen_now():
        ready = sorted((g for g in left if g in complete), key=complete.get)
        return choose(ready, ROWS // HALF) if sum(len(groups[g]) for g in ready) >= ROWS // HALF else None

    for what, length in segments:
        acts = []
        if what in ("part", "kvL"):
            now = max(now, tokens_at.pop())
        send_ready(acts)
        if not actions:
            free["x"] += 9.0
        while True:
            soon = [(t, m) for t, m in pending() if t <= now - margin]
            if not soon:
                break
            take(soon[0][1], acts)
        if what in ("step", "ahead"):
            while (chosen := chosen_now()) is None:
                take(pending()[0][1], acts)
            for g in chosen:
                left.remove(g)
            order.append(chosen)
        actions.append((what, acts))
        now += length
        if what == "kvL":
            have.update([("L1", 0, 0, 0), ("L2", 0, 0, 0)])
    assert not left and len(arrived) == len(messages)
    place = {}
    for chunk, chosen in enumerate(order):
        row = 0
        for g in chosen:
            for item in groups[g]:
                place[item] = (chunk, row)
                row += HALF
        assert row == ROWS
    return messages, actions, place, now


MESSAGES, ACTIONS, PLACE, ESTIMATE = plan()


def kernel(
    tok_in, wq_in, wk_in, wv_in, blocks, base, offset, out,
    tok, wq, wkv, query, kv, aug, largest, acc, late,
    send, recv, tok_sem, relay_sem, local,
):
    ctx, head = lax.axis_index("ctx"), lax.axis_index("head")
    x, y, z = ctx // 32, (ctx // 8) % 4, ctx % 8
    early, core = head // 2, head % 2

    def device(x, y, z):
        return ((x * 4 + y) * 8 + z, head)

    near = {
        "x": device(1 - x, y, z),
        "y+": device(x, (y + 1) % 4, z),
        "y-": device(x, (y + 3) % 4, z),
        "z+": device(x, y, (z + 1) % 8),
        "z-": device(x, y, (z + 7) % 8),
        "y2": device(x, (y + 2) % 4, z),
        "z+2": device(x, y, (z + 2) % 8),
        "z-2": device(x, y, (z + 6) % 8),
    }
    beside = (ctx, head + 1 - 2 * core)
    across = (ctx, (head + 2) % 4)

    barrier = pltpu.get_barrier_semaphore()
    peers = list(near.values()) + [beside, across]
    for peer in peers:
        pl.semaphore_signal(barrier, inc=1, device_id=peer, device_id_type=pl.DeviceIdType.MESH)

    mine = pl.ds(pl.multiple_of(core * 64, 64), 64)
    own_tokens = pltpu.make_async_copy(tok_in, tok.at[0, mine], local.at[2])
    own_tokens.start()
    copies = [
        pltpu.make_async_copy(wk_in, wkv.at[:, 0:HD], local.at[0]),
        pltpu.make_async_copy(wv_in, wkv.at[:, HD : 2 * HD], local.at[1]),
    ]
    for copy in copies:
        copy.start()
    wide = []
    for j in range(4):
        columns = pl.ds(j * WIDE, WIDE)
        wide.append(pltpu.make_async_copy(wq_in.at[:, columns], wq.at[:, columns], local.at[3 + j]))
        wide[-1].start()
    pl.semaphore_wait(barrier, len(peers))

    def remote(src, dst, s, r, to):
        return pltpu.make_async_remote_copy(
            src_ref=src, dst_ref=dst, send_sem=s, recv_sem=r, device_id=to,
            device_id_type=pl.DeviceIdType.MESH,
        )

    to_beside = remote(tok_in, tok.at[0, mine], tok_sem.at[0], tok_sem.at[1], beside)
    to_beside.start()
    to_across, relays = [], []
    for j in range(4):
        piece = pl.ds(j * ROWS, ROWS)
        to_across.append(
            remote(tok_in.at[:, piece], tok.at[1, mine, piece], tok_sem.at[2 + j], tok_sem.at[6 + j], across)
        )
        relays.append(
            remote(tok.at[1, mine, piece], tok.at[1, mine, piece], relay_sem.at[j], relay_sem.at[4 + j], beside)
        )
    to_across[0].start()

    own = [blocks[ctx * 2 + early], blocks[ctx * 2 + 1 - early]]

    def mask_blocks():
        lanes = lax.broadcasted_iota(jnp.int32, (16, HD), 1)
        bound = jnp.where(lanes == 0, own[0], jnp.where(lanes == 1, own[1], 1 << 20))
        for dx in range(NX):
            for dy in range(NY):
                for dz in range(NZ):
                    origin = (((x + dx) % NX) * 4 + (y - dy + NY) % NY) * 8 + (z - dz + NZ) % NZ
                    for part, kinds in ((early, KINDS["E"]), (1 - early, KINDS["L"])):
                        place = blocks[origin * 2 + part]
                        mask = jnp.where(place < bound, 0.0, LOW).astype(jnp.bfloat16)
                        for kind in kinds:
                            chunk, row = PLACE[(kind, dx, dy, dz)]
                            aug[chunk, row // HALF] = mask

    def slot(items):
        chunk, row = PLACE[items[0]]
        count = len(items) * HALF
        spots = [PLACE[item] for item in items]
        assert spots == [(chunk, row + n * HALF) for n in range(len(items))]
        return kv.at[chunk, :, pl.ds(row, count)]

    def message(m):
        way, items = MESSAGES[m]
        landing = [moved(item, way) for item in items]
        return remote(slot(items), slot(landing), send.at[m], recv.at[m], near[way])

    def communicate(acts):
        for what, m in acts:
            if what == "send":
                message(m).start()
            else:
                message(m).wait_recv()

    def rotation(part):
        turn = own[part]
        base_cos, base_sin = base[0, pl.ds(turn, 1)], base[1, pl.ds(turn, 1)]
        cosine = base_cos * offset[0] - base_sin * offset[1]
        sine = base_sin * offset[0] + base_cos * offset[1]
        return lambda values: (values * cosine + pltpu.roll(values, HD // 2, 1) * sine).astype(jnp.bfloat16)

    spots = [[(kind, 0, 0, 0) for kind in KINDS[part]] for part in "EL"]

    def store_kv(part, both):
        keys, values = rotation(part)(both[:, :HD]), both[:, HD:].astype(jnp.bfloat16)
        size = BLK // len(spots[part])
        for n, item in enumerate(spots[part]):
            chunk, row = PLACE[item]
            kv[chunk, 0, pl.ds(row, size)] = keys[n * size : (n + 1) * size]
            kv[chunk, 1, pl.ds(row, size)] = values[n * size : (n + 1) * size]

    def store_q(part, j, both):
        rotate = rotation(part)
        for h in range(2):
            rows = pl.ds(part * ROWS + (2 * j + h) * BLK, BLK)
            query[rows] = rotate(both[:, h * HD : (h + 1) * HD])

    def late_part(k, js):
        piece = pl.ds(k * ROWS, ROWS)
        for j in js:
            weights = wkv[piece] if j == 4 else wq[piece, j * WIDE : (j + 1) * WIDE]
            product = jnp.dot(tok[1, :, piece], weights, preferred_element_type=jnp.float32)
            if k:
                product = late[j] + product
            if k < 3:
                late[j] = product
            elif j == 4:
                store_kv(1, product)
            else:
                store_q(1, j, product)

    lane = lax.broadcasted_iota(jnp.int32, (TILE, HD), 1)
    marks = [jnp.where(lane == part, 1.0, 0.0).astype(jnp.bfloat16) for part in range(2)]

    def own_block(part):
        ones = jnp.ones((BLK, HD), jnp.bfloat16)
        row = lax.broadcasted_iota(jnp.int32, (TILE, BLK), 0) % BLK
        keep = lax.broadcasted_iota(jnp.int32, (TILE, BLK), 1) <= row
        size = BLK // len(spots[part])
        at = [PLACE[item] for item in spots[part]]
        keys, values = (
            jnp.concatenate([kv[chunk, n, pl.ds(row, size)] for chunk, row in at], 0) for n in range(2)
        )
        values = jnp.concatenate([values, ones], 1)
        for t in range(ROWS // TILE):
            rows = pl.ds(part * ROWS + t * TILE, TILE)
            scores = lax.dot_general(query[rows], keys, CONTRACT_LAST, preferred_element_type=jnp.float32)
            scores = jnp.where(keep, scores, LOW)
            top = jnp.broadcast_to(jnp.max(scores, axis=1, keepdims=True), (TILE, HD))
            expo = jnp.exp2((scores - top) * FACTOR).astype(jnp.bfloat16)
            largest[rows] = top
            acc[rows] = jnp.dot(expo, values, preferred_element_type=jnp.float32)

    def score(part, rows, chunk):
        masks = [aug[chunk, b] for b in range(ROWS // HALF) for _ in range(HALF // 16)]
        keys = jnp.concatenate([kv[chunk, 0], jnp.concatenate(masks, 0)], 1)
        wide_query = jnp.concatenate([query[rows], marks[part]], 1)
        return lax.dot_general(wide_query, keys, CONTRACT_LAST, preferred_element_type=jnp.float32)

    def weigh(rows, scores):
        before = largest[rows]
        after = jnp.maximum(before, jnp.max(scores, axis=1, keepdims=True))
        largest[rows] = after
        expo = [
            jnp.exp2((scores[:, n : n + HD] - after) * FACTOR).astype(jnp.bfloat16) for n in range(0, ROWS, HD)
        ]
        return jnp.concatenate(expo, 1), jnp.exp2((before - after) * FACTOR)

    def gather(rows, chunk, expo, shrink):
        values = jnp.concatenate([kv[chunk, 1], jnp.ones((ROWS, HD), jnp.bfloat16)], 1)
        product = jnp.dot(expo, values, preferred_element_type=jnp.float32)
        acc[rows] = acc[rows] * jnp.concatenate([shrink, shrink], 1) + product

    def attend(pairs):
        work = [
            (part, pl.ds(part * ROWS + t * TILE, TILE), chunk) for part, chunk in pairs for t in range(ROWS // TILE)
        ]
        scores, weights = {}, {}
        for n in range(len(work) + 2):
            if n < len(work):
                scores[n] = score(*work[n])
            if n >= 2:
                part, rows, chunk = work[n - 2]
                gather(rows, chunk, *weights.pop(n - 2))
            if 1 <= n <= len(work):
                weights[n - 1] = weigh(work[n - 1][1], scores.pop(n - 1))

    own_tokens.wait()
    to_beside.wait_recv()
    for copy in copies:
        copy.wait()
    store_kv(0, jnp.dot(tok[0], wkv[...], preferred_element_type=jnp.float32))
    step_acts = []
    count = {what: 0 for what, _ in ACTIONS}
    for what, acts in ACTIONS:
        n = count[what]
        count[what] += 1
        if what == "step":
            step_acts.append(acts)
            continue
        communicate(acts)
        if what == "qE" and n == 0:
            for k in range(1, 4):
                to_across[k].start()
            mask_blocks()
        if what == "qE":
            wide[n].wait()
            columns = slice(n * WIDE, (n + 1) * WIDE)
            store_q(0, n, jnp.dot(tok[0], wq[:, columns], preferred_element_type=jnp.float32))
        elif what == "ownE":
            own_block(0)
        elif what == "ahead":
            attend([(0, n)])
        elif what == "part":
            to_across[n].wait_recv()
            relays[n].start()
            if n:
                relays[n - 1].wait_recv()
                late_part(n - 1, range(5))
        elif what == "kvL":
            to_across[3].wait_recv()
            relays[3].start()
            relays[2].wait_recv()
            late_part(2, range(5))
            relays[3].wait_recv()
            late_part(3, [4])
        elif what == "qL":
            late_part(3, range(4))
        else:
            own_block(1)

    def one_step(step, carry):
        def pick(low, high):
            if high - low == 1:
                communicate(step_acts[low])
            else:
                middle = (low + high) // 2
                lax.cond(step < middle, lambda: pick(low, middle), lambda: pick(middle, high))

        pick(0, len(step_acts))
        attend([(1, step), (0, step + AHEAD)])
        return carry

    lax.fori_loop(0, CHUNKS - AHEAD, one_step, 0)
    attend([(1, chunk) for chunk in range(CHUNKS - AHEAD, CHUNKS)])

    for part in range(2):
        block = pl.ds(pl.multiple_of((early if part == 0 else 1 - early) * BLK, BLK), BLK)
        for h in range(8):
            rows = pl.ds(part * ROWS + h * BLK, BLK)
            total = acc[rows]
            out[block, h * HD : (h + 1) * HD] = (total[:, :HD] / total[:, HD:]).astype(jnp.bfloat16)

    for m in range(len(MESSAGES)):
        message(m).wait_send()
    to_beside.wait_send()
    for k in range(4):
        to_across[k].wait_send()
        relays[k].wait_send()


def rotary_tables():
    freqs = 500000.0 ** (-(np.arange(HD // 2) * 2.0) / HD)
    out = []
    for positions in (np.arange(128.0) * BLK, np.arange(float(BLK))):
        angles = positions[:, None] * freqs[None, :]
        cosine, sine = np.cos(angles), np.sin(angles)
        joined = [np.concatenate([cosine, cosine], 1), np.concatenate([-sine, sine], 1)]
        out.append(jnp.asarray(np.stack(joined), jnp.float32))
    return out


def per_device(tokens, w_query, w_key, w_value, block_order):
    anywhere, vmem = pl.BlockSpec(memory_space=pl.ANY), pl.BlockSpec(memory_space=pltpu.VMEM)
    count = len(MESSAGES)
    return pl.pallas_call(
        kernel,
        out_shape=jax.ShapeDtypeStruct((256, 1024), jnp.bfloat16),
        in_specs=[anywhere] * 4 + [pl.BlockSpec(memory_space=pltpu.SMEM), vmem, vmem],
        out_specs=vmem,
        scratch_shapes=[
            pltpu.VMEM((2, 128, 4096), jnp.bfloat16),
            pltpu.VMEM((4096, 1024), jnp.bfloat16),
            pltpu.VMEM((4096, 256), jnp.bfloat16),
            pltpu.VMEM((2048, HD), jnp.bfloat16),
            pltpu.VMEM((CHUNKS, 2, ROWS, HD), jnp.bfloat16),
            pltpu.VMEM((CHUNKS, ROWS // HALF, 16, HD), jnp.bfloat16),
            pltpu.VMEM((2048, HD), jnp.float32),
            pltpu.VMEM((2048, 2 * HD), jnp.float32),
            pltpu.VMEM((5, BLK, WIDE), jnp.float32),
            pltpu.SemaphoreType.DMA((count,)),
            pltpu.SemaphoreType.DMA((count,)),
            pltpu.SemaphoreType.DMA((10,)),
            pltpu.SemaphoreType.DMA((8,)),
            pltpu.SemaphoreType.DMA((7,)),
        ],
        compiler_params=pltpu.CompilerParams(
            collective_id=0, has_side_effects=True, vmem_limit_bytes=56 << 20
        ),
        cost_estimate=pl.CostEstimate(flops=38 * 10**9, bytes_accessed=12 * 10**6, transcendentals=33 * 10**6),
    )(tokens, w_query, w_key, w_value, block_order, *rotary_tables())


def solution(mesh):
    return jax.shard_map(
        per_device,
        mesh=mesh,
        in_specs=(P(("ctx", "head"), None), P(None, "head"), P(None, "head"), P(None, "head"), P()),
        out_specs=P("ctx", "head"),
        check_vma=False,
    )
```

```python
import math

import jax
import jax.numpy as jnp
import numpy as np
from jax import lax
from jax.experimental import pallas as pl
from jax.experimental.pallas import tpu as pltpu
from jax.sharding import PartitionSpec as P

HD = 128
BLK = 128
NX, NY, NZ = 2, 4, 8
CHUNKS = 16
ROWS = 1024
HALF = 64
TILE = 1024
WIDE = 256
AHEAD = 0
LOW = -1e30
FACTOR = math.log2(math.e) / math.sqrt(HD)
CONTRACT_LAST = (((1,), (1,)), ((), ()))
MOVES = {
    "x": (1, 0, 0), "y+": (0, 1, 0), "y-": (0, -1, 0), "z+": (0, 0, 1), "z-": (0, 0, -1),
    "y2": (0, 2, 0), "z+2": (0, 0, 2), "z-2": (0, 0, -2),
}
LOADS = {"y2": {"y+": 1, "y-": 1}, "z+2": {"z+": 2}, "z-2": {"z-": 2}}
KINDS = {"E": ("E1", "E2"), "L": ("L1", "L2")}
YS = (0, 1, 3, 2)
ZS = (0, 1, 7, 2, 6, 3, 5, 4)
BACKLOG = 3.0
PATHS = {"E1": "xzy", "E2": "yzx", "L1": "xzy", "L2": "xyz"}
FAR = ("E1", "E2", "L1", "L2",)
FIRST = [
    ("E2", "x"), ("L2", "y"), ("L2", "x"), ("E1", "y"), ("L1", "x"), ("E1", "x"),
    ("L2", "z"), ("L1", "z"), ("E2", "z"), ("E2", "y"), ("L1", "y"), ("E1", "z"),
]


def moved(item, way):
    kind, x, y, z = item
    dx, dy, dz = MOVES[way]
    return (kind, (x + dx) % NX, (y + dy) % NY, (z + dz) % NZ)


def run(kind, xs, ys, zs):
    return [(kind, x, y, z) for y in ys for z in zs for x in xs]


def all_groups():
    out = []
    for kind, path in PATHS.items():
        sides = [(0, 1)] if path[0] == "x" else [(0,), (1,)]
        for xs in sides:
            if path.index("y") < path.index("z"):
                for z in range(NZ):
                    out += [run(kind, xs, ys, (z,)) for ys in (YS[:2], YS[2:])]
            else:
                for y in range(NY):
                    out += [run(kind, xs, (y,), ZS[n : n + 2]) for n in (0, 2, 4, 6)]
    return out


def first_y(kind, xs, far):
    out = [(way, run(kind, (x,), (0,), (0,))) for x in xs for way in ("y+", "y-")]
    if far:
        return out + [("y2", run(kind, (x,), (0,), (0,))) for x in xs]
    out.append(("y+", run(kind, (0,), (1,), (0,))))
    return out + ([("y-", run(kind, (1,), (3,), (0,)))] if len(xs) > 1 else [])


def first_z(kind, xs, far):
    out = [(way, run(kind, (x,), (0,), (0,))) for x in xs for way in ("z+", "z-")]
    if far:
        out += [(way, run(kind, (x,), (0,), (0,))) for x in xs for way in ("z+2", "z-2")]
        out += [("z+", run(kind, xs, (0,), (2,))), ("z-", run(kind, xs, (0,), (6,)))]
        out.append(("z+2", run(kind, (0,), (0,), (2,))))
        return out + ([("z-2", run(kind, (1,), (0,), (6,)))] if len(xs) > 1 else [])
    for up, down in ((1, 7), (2, 6)):
        out += [("z+", run(kind, xs, (0,), (up,))), ("z-", run(kind, xs, (0,), (down,)))]
    out.append(("z+", run(kind, (0,), (0,), (3,))))
    return out + ([("z-", run(kind, (1,), (0,), (5,)))] if len(xs) > 1 else [])


def along_z(kind, xs):
    out = []
    for up, down in ((0, 0), (1, 7), (2, 6)):
        for ys in (YS[:1], YS[1:2], YS[2:]):
            out += [("z+", run(kind, xs, ys, (up,))), ("z-", run(kind, xs, ys, (down,)))]
    out.append(("z+", run(kind, xs, YS[:2], (3,))))
    return out + [("z-", run(kind, xs, YS[2:], (5,)))]


def along_y(kind, xs):
    out = []
    for zs in (ZS[:1], ZS[1:2], ZS[2:4], ZS[4:6], ZS[6:]):
        out += [(way, run(kind, xs, (0,), zs)) for way in ("y+", "y-")]
    for zs in (ZS[:2], ZS[2:4]):
        out.append(("y+", run(kind, xs, (1,), zs)))
    for zs in (ZS[4:6], ZS[6:]):
        out.append(("y-", run(kind, xs, (3,), zs)))
    return out


def stages(kind):
    path, both = PATHS[kind], (0, 1)
    xs = both if path[0] == "x" else (0,)
    if path.index("y") < path.index("z"):
        first, then = ("y", first_y(kind, xs, kind in FAR)), ("z", along_z(kind, xs))
        rows = [run(kind, (0,), ys, (z,)) for z in ZS for ys in (YS[:2], YS[2:])]
    else:
        first, then = ("z", first_z(kind, xs, kind in FAR)), ("y", along_y(kind, xs))
        rows = [run(kind, (0,), (y,), ZS[n : n + 2]) for y in YS for n in (0, 2, 4, 6)]
    if path[0] == "x":
        rows = [run(kind, (0,), (0,), (0,))]
    return dict([first, then, ("x", [("x", items) for items in rows])])


def all_messages():
    return [message for kind, axis in FIRST for message in stages(kind)[axis]]


def plan():
    messages, groups = all_messages(), all_groups()
    half_us, latency, issue_us, margin = 0.82, 2.8, 0.02, 0.4
    segments = [("qE", 0.6)] * 4 + [("ownE", 0.4)] + [("part", 0.8)] * 3 + [("ahead", 1.4)] * AHEAD
    segments += [("kvL", 0.5), ("qL", 1.2), ("ownL", 0.4)]
    segments += [("step", 2.75)] * (CHUNKS - AHEAD)
    tokens_at = [16.0, 12.5, 9.5, 6.5]
    have = {("E1", 0, 0, 0), ("E2", 0, 0, 0)}
    free = {way: 0.0 for way in MOVES if way not in LOADS}
    arrival, unsent, arrived, left = {}, list(range(len(messages))), set(), list(range(len(groups)))
    complete = {}
    now = 2.5
    actions, order = [], []

    def send_ready(acts):
        nonlocal now
        for m in list(unsent):
            way, items = messages[m]
            loads = LOADS.get(way, {way: 1})
            start = max(free[link] for link in loads)
            if start <= now + BACKLOG and all(item in have for item in items):
                unsent.remove(m)
                now += issue_us
                start = max(now, start)
                for link, load in loads.items():
                    free[link] = start + half_us * len(items) * load
                arrival[m] = max(free[link] for link in loads) + latency + (0.7 if way in LOADS else 0.0)
                acts.append(("send", m))

    def note():
        for g in left:
            if g not in complete and all(item in have for item in groups[g]):
                complete[g] = len(complete)

    def take(m, acts):
        nonlocal now
        acts.append(("wait", m))
        now = max(now, arrival[m]) + issue_us
        arrived.add(m)
        have.update(moved(item, messages[m][0]) for item in messages[m][1])
        note()
        send_ready(acts)

    def pending():
        return sorted((arrival[m], m) for m in arrival if m not in arrived)

    def choose(ready, room):
        if room == 0:
            return []
        for n, g in enumerate(ready):
            if len(groups[g]) <= room:
                rest = choose(ready[n + 1 :], room - len(groups[g]))
                if rest is not None:
                    return [g] + rest
        return None

    def chosen_now():
        ready = sorted((g for g in left if g in complete), key=complete.get)
        return choose(ready, ROWS // HALF) if sum(len(groups[g]) for g in ready) >= ROWS // HALF else None

    for what, length in segments:
        acts = []
        if what in ("part", "kvL"):
            now = max(now, tokens_at.pop())
        send_ready(acts)
        if not actions:
            free["x"] += 9.0
        while True:
            soon = [(t, m) for t, m in pending() if t <= now - margin]
            if not soon:
                break
            take(soon[0][1], acts)
        if what in ("step", "ahead"):
            while (chosen := chosen_now()) is None:
                take(pending()[0][1], acts)
            for g in chosen:
                left.remove(g)
            order.append(chosen)
        actions.append((what, acts))
        now += length
        if what == "kvL":
            have.update([("L1", 0, 0, 0), ("L2", 0, 0, 0)])
    assert not left and len(arrived) == len(messages)
    place = {}
    for chunk, chosen in enumerate(order):
        row = 0
        for g in chosen:
            for item in groups[g]:
                place[item] = (chunk, row)
                row += HALF
        assert row == ROWS
    return messages, actions, place, now


MESSAGES, ACTIONS, PLACE, ESTIMATE = plan()


def kernel(
    tok_in, wq_in, wk_in, wv_in, blocks, base, offset, out,
    tok, wq, wkv, query, kv, aug, largest, acc, late,
    send, recv, tok_sem, relay_sem, local,
):
    ctx, head = lax.axis_index("ctx"), lax.axis_index("head")
    x, y, z = ctx // 32, (ctx // 8) % 4, ctx % 8
    early, core = head // 2, head % 2

    def device(x, y, z):
        return ((x * 4 + y) * 8 + z, head)

    near = {
        "x": device(1 - x, y, z),
        "y+": device(x, (y + 1) % 4, z),
        "y-": device(x, (y + 3) % 4, z),
        "z+": device(x, y, (z + 1) % 8),
        "z-": device(x, y, (z + 7) % 8),
        "y2": device(x, (y + 2) % 4, z),
        "z+2": device(x, y, (z + 2) % 8),
        "z-2": device(x, y, (z + 6) % 8),
    }
    beside = (ctx, head + 1 - 2 * core)
    across = (ctx, (head + 2) % 4)

    barrier = pltpu.get_barrier_semaphore()
    peers = list(near.values()) + [beside, across]
    for peer in peers:
        pl.semaphore_signal(barrier, inc=1, device_id=peer, device_id_type=pl.DeviceIdType.MESH)

    mine = pl.ds(pl.multiple_of(core * 64, 64), 64)
    own_tokens = pltpu.make_async_copy(tok_in, tok.at[0, mine], local.at[2])
    own_tokens.start()
    copies = [
        pltpu.make_async_copy(wk_in, wkv.at[:, 0:HD], local.at[0]),
        pltpu.make_async_copy(wv_in, wkv.at[:, HD : 2 * HD], local.at[1]),
    ]
    for copy in copies:
        copy.start()
    wide = []
    for j in range(4):
        columns = pl.ds(j * WIDE, WIDE)
        wide.append(pltpu.make_async_copy(wq_in.at[:, columns], wq.at[:, columns], local.at[3 + j]))
        wide[-1].start()
    pl.semaphore_wait(barrier, len(peers))

    def remote(src, dst, s, r, to):
        return pltpu.make_async_remote_copy(
            src_ref=src, dst_ref=dst, send_sem=s, recv_sem=r, device_id=to,
            device_id_type=pl.DeviceIdType.MESH,
        )

    to_beside = remote(tok_in, tok.at[0, mine], tok_sem.at[0], tok_sem.at[1], beside)
    to_beside.start()
    to_across, relays = [], []
    for j in range(4):
        piece = pl.ds(j * ROWS, ROWS)
        to_across.append(
            remote(tok_in.at[:, piece], tok.at[1, mine, piece], tok_sem.at[2 + j], tok_sem.at[6 + j], across)
        )
        relays.append(
            remote(tok.at[1, mine, piece], tok.at[1, mine, piece], relay_sem.at[j], relay_sem.at[4 + j], beside)
        )
    to_across[0].start()

    own = [blocks[ctx * 2 + early], blocks[ctx * 2 + 1 - early]]

    def mask_blocks():
        lanes = lax.broadcasted_iota(jnp.int32, (16, HD), 1)
        bound = jnp.where(lanes == 0, own[0], jnp.where(lanes == 1, own[1], 1 << 20))
        for dx in range(NX):
            for dy in range(NY):
                for dz in range(NZ):
                    origin = (((x + dx) % NX) * 4 + (y - dy + NY) % NY) * 8 + (z - dz + NZ) % NZ
                    for part, kinds in ((early, KINDS["E"]), (1 - early, KINDS["L"])):
                        place = blocks[origin * 2 + part]
                        mask = jnp.where(place < bound, 0.0, LOW).astype(jnp.bfloat16)
                        for kind in kinds:
                            chunk, row = PLACE[(kind, dx, dy, dz)]
                            aug[chunk, row // HALF] = mask

    def slot(items):
        chunk, row = PLACE[items[0]]
        count = len(items) * HALF
        spots = [PLACE[item] for item in items]
        assert spots == [(chunk, row + n * HALF) for n in range(len(items))]
        return kv.at[chunk, :, pl.ds(row, count)]

    def message(m):
        way, items = MESSAGES[m]
        landing = [moved(item, way) for item in items]
        return remote(slot(items), slot(landing), send.at[m], recv.at[m], near[way])

    def communicate(acts):
        for what, m in acts:
            if what == "send":
                message(m).start()
            else:
                message(m).wait_recv()

    def rotation(part):
        turn = own[part]
        base_cos, base_sin = base[0, pl.ds(turn, 1)], base[1, pl.ds(turn, 1)]
        cosine = base_cos * offset[0] - base_sin * offset[1]
        sine = base_sin * offset[0] + base_cos * offset[1]
        return lambda values: (values * cosine + pltpu.roll(values, HD // 2, 1) * sine).astype(jnp.bfloat16)

    spots = [[(kind, 0, 0, 0) for kind in KINDS[part]] for part in "EL"]

    def store_kv(part, both):
        keys, values = rotation(part)(both[:, :HD]), both[:, HD:].astype(jnp.bfloat16)
        size = BLK // len(spots[part])
        for n, item in enumerate(spots[part]):
            chunk, row = PLACE[item]
            kv[chunk, 0, pl.ds(row, size)] = keys[n * size : (n + 1) * size]
            kv[chunk, 1, pl.ds(row, size)] = values[n * size : (n + 1) * size]

    def store_q(part, j, both):
        rotate = rotation(part)
        for h in range(2):
            rows = pl.ds(part * ROWS + (2 * j + h) * BLK, BLK)
            query[rows] = rotate(both[:, h * HD : (h + 1) * HD])

    def late_part(k, js):
        piece = pl.ds(k * ROWS, ROWS)
        for j in js:
            weights = wkv[piece] if j == 4 else wq[piece, j * WIDE : (j + 1) * WIDE]
            product = jnp.dot(tok[1, :, piece], weights, preferred_element_type=jnp.float32)
            if k:
                product = late[j] + product
            if k < 3:
                late[j] = product
            elif j == 4:
                store_kv(1, product)
            else:
                store_q(1, j, product)

    lane = lax.broadcasted_iota(jnp.int32, (TILE, HD), 1)
    marks = [jnp.where(lane == part, 1.0, 0.0).astype(jnp.bfloat16) for part in range(2)]

    def own_block(part):
        ones = jnp.ones((BLK, HD), jnp.bfloat16)
        row = lax.broadcasted_iota(jnp.int32, (TILE, BLK), 0) % BLK
        keep = lax.broadcasted_iota(jnp.int32, (TILE, BLK), 1) <= row
        size = BLK // len(spots[part])
        at = [PLACE[item] for item in spots[part]]
        keys, values = (
            jnp.concatenate([kv[chunk, n, pl.ds(row, size)] for chunk, row in at], 0) for n in range(2)
        )
        values = jnp.concatenate([values, ones], 1)
        for t in range(ROWS // TILE):
            rows = pl.ds(part * ROWS + t * TILE, TILE)
            scores = lax.dot_general(query[rows], keys, CONTRACT_LAST, preferred_element_type=jnp.float32)
            scores = jnp.where(keep, scores, LOW)
            top = jnp.broadcast_to(jnp.max(scores, axis=1, keepdims=True), (TILE, HD))
            expo = jnp.exp2((scores - top) * FACTOR).astype(jnp.bfloat16)
            largest[rows] = top
            acc[rows] = jnp.dot(expo, values, preferred_element_type=jnp.float32)

    def score(part, rows, chunk):
        masks = [aug[chunk, b] for b in range(ROWS // HALF) for _ in range(HALF // 16)]
        keys = jnp.concatenate([kv[chunk, 0], jnp.concatenate(masks, 0)], 1)
        wide_query = jnp.concatenate([query[rows], marks[part]], 1)
        return lax.dot_general(wide_query, keys, CONTRACT_LAST, preferred_element_type=jnp.float32)

    def weigh(rows, scores):
        before = largest[rows]
        after = jnp.maximum(before, jnp.max(scores, axis=1, keepdims=True))
        largest[rows] = after
        expo = [
            jnp.exp2((scores[:, n : n + HD] - after) * FACTOR).astype(jnp.bfloat16) for n in range(0, ROWS, HD)
        ]
        return jnp.concatenate(expo, 1), jnp.exp2((before - after) * FACTOR)

    def gather(rows, chunk, expo, shrink):
        values = jnp.concatenate([kv[chunk, 1], jnp.ones((ROWS, HD), jnp.bfloat16)], 1)
        product = jnp.dot(expo, values, preferred_element_type=jnp.float32)
        acc[rows] = acc[rows] * jnp.concatenate([shrink, shrink], 1) + product

    def attend(pairs):
        work = [
            (part, pl.ds(part * ROWS + t * TILE, TILE), chunk) for part, chunk in pairs for t in range(ROWS // TILE)
        ]
        scores, weights = {}, {}
        for n in range(len(work) + 2):
            if n < len(work):
                scores[n] = score(*work[n])
            if n >= 2:
                part, rows, chunk = work[n - 2]
                gather(rows, chunk, *weights.pop(n - 2))
            if 1 <= n <= len(work):
                weights[n - 1] = weigh(work[n - 1][1], scores.pop(n - 1))

    own_tokens.wait()
    to_beside.wait_recv()
    for copy in copies:
        copy.wait()
    store_kv(0, jnp.dot(tok[0], wkv[...], preferred_element_type=jnp.float32))
    step_acts = []
    count = {what: 0 for what, _ in ACTIONS}
    for what, acts in ACTIONS:
        n = count[what]
        count[what] += 1
        if what == "step":
            step_acts.append(acts)
            continue
        communicate(acts)
        if what == "qE" and n == 0:
            for k in range(1, 4):
                to_across[k].start()
            mask_blocks()
        if what == "qE":
            wide[n].wait()
            columns = slice(n * WIDE, (n + 1) * WIDE)
            store_q(0, n, jnp.dot(tok[0], wq[:, columns], preferred_element_type=jnp.float32))
        elif what == "ownE":
            own_block(0)
        elif what == "ahead":
            attend([(0, n)])
        elif what == "part":
            to_across[n].wait_recv()
            relays[n].start()
            if n:
                relays[n - 1].wait_recv()
                late_part(n - 1, range(5))
        elif what == "kvL":
            to_across[3].wait_recv()
            relays[3].start()
            relays[2].wait_recv()
            late_part(2, range(5))
            relays[3].wait_recv()
            late_part(3, [4])
        elif what == "qL":
            late_part(3, range(4))
        else:
            own_block(1)

    def one_step(step, carry):
        def pick(low, high):
            if high - low == 1:
                communicate(step_acts[low])
            else:
                middle = (low + high) // 2
                lax.cond(step < middle, lambda: pick(low, middle), lambda: pick(middle, high))

        pick(0, len(step_acts))
        attend([(1, step), (0, step + AHEAD)])
        return carry

    lax.fori_loop(0, CHUNKS - AHEAD, one_step, 0)
    attend([(1, chunk) for chunk in range(CHUNKS - AHEAD, CHUNKS)])

    for part in range(2):
        block = pl.ds(pl.multiple_of((early if part == 0 else 1 - early) * BLK, BLK), BLK)
        for h in range(8):
            rows = pl.ds(part * ROWS + h * BLK, BLK)
            total = acc[rows]
            out[block, h * HD : (h + 1) * HD] = (total[:, :HD] / total[:, HD:]).astype(jnp.bfloat16)

    for m in range(len(MESSAGES)):
        message(m).wait_send()
    to_beside.wait_send()
    for k in range(4):
        to_across[k].wait_send()
        relays[k].wait_send()


def rotary_tables():
    freqs = 500000.0 ** (-(np.arange(HD // 2) * 2.0) / HD)
    out = []
    for positions in (np.arange(128.0) * BLK, np.arange(float(BLK))):
        angles = positions[:, None] * freqs[None, :]
        cosine, sine = np.cos(angles), np.sin(angles)
        joined = [np.concatenate([cosine, cosine], 1), np.concatenate([-sine, sine], 1)]
        out.append(jnp.asarray(np.stack(joined), jnp.float32))
    return out


def per_device(tokens, w_query, w_key, w_value, block_order):
    anywhere, vmem = pl.BlockSpec(memory_space=pl.ANY), pl.BlockSpec(memory_space=pltpu.VMEM)
    count = len(MESSAGES)
    return pl.pallas_call(
        kernel,
        out_shape=jax.ShapeDtypeStruct((256, 1024), jnp.bfloat16),
        in_specs=[anywhere] * 4 + [pl.BlockSpec(memory_space=pltpu.SMEM), vmem, vmem],
        out_specs=vmem,
        scratch_shapes=[
            pltpu.VMEM((2, 128, 4096), jnp.bfloat16),
            pltpu.VMEM((4096, 1024), jnp.bfloat16),
            pltpu.VMEM((4096, 256), jnp.bfloat16),
            pltpu.VMEM((2048, HD), jnp.bfloat16),
            pltpu.VMEM((CHUNKS, 2, ROWS, HD), jnp.bfloat16),
            pltpu.VMEM((CHUNKS, ROWS // HALF, 16, HD), jnp.bfloat16),
            pltpu.VMEM((2048, HD), jnp.float32),
            pltpu.VMEM((2048, 2 * HD), jnp.float32),
            pltpu.VMEM((5, BLK, WIDE), jnp.float32),
            pltpu.SemaphoreType.DMA((count,)),
            pltpu.SemaphoreType.DMA((count,)),
            pltpu.SemaphoreType.DMA((10,)),
            pltpu.SemaphoreType.DMA((8,)),
            pltpu.SemaphoreType.DMA((7,)),
        ],
        compiler_params=pltpu.CompilerParams(
            collective_id=0, has_side_effects=True, vmem_limit_bytes=56 << 20
        ),
        cost_estimate=pl.CostEstimate(flops=38 * 10**9, bytes_accessed=12 * 10**6, transcendentals=33 * 10**6),
    )(tokens, w_query, w_key, w_value, block_order, *rotary_tables())


def solution(mesh):
    return jax.shard_map(
        per_device,
        mesh=mesh,
        in_specs=(P(("ctx", "head"), None), P(None, "head"), P(None, "head"), P(None, "head"), P()),
        out_specs=P("ctx", "head"),
        check_vma=False,
    )
```
